512 devices in a mesh: sy: 8 (over z_hi, y), sz: 16 (over z_lo, core), filt: 4 (over x).
Axes of the slice: x: 4, y: 4, z: 16 (z_hi: 2, z_lo: 8; z = z_hi * 8 + z_lo), core: 2. Of those that a mesh axis runs over, the one named last changes fastest.
Arguments:
- volume: bfloat16 [64, 16, 64, 128], P('filt', 'sy', 'sz'), may hold values from -6 to 6
- first_filters: bfloat16 [64, 1728], P('filt'), may hold values from -0.15625 to 0.15625
- second_filters: bfloat16 [64, 1728], P('filt'), may hold values from -0.15625 to 0.15625
- cotangent: bfloat16 [64, 16, 64, 128], P('filt', 'sy', 'sz'), may hold values from -6 to 6
Outputs:
- result: bfloat16 [64, 16, 64, 128], P('filt', 'sy', 'sz')
- grad_input: bfloat16 [64, 16, 64, 128], P('filt', 'sy', 'sz')
- first_grad: float32 [64, 1728], P('filt')
- second_grad: float32 [64, 1728], P('filt')
The draws below stay inside these ranges and needn't reach their ends.
All inputs are finite; a program needn't handle non-finite values.
Results may differ from the reference program's by a relative error of at most 0.0075.
Values may be sent and summed in bfloat16 or wider, within the bound.
No kernel may reach another device: no remote copies, remote signals or barrier semaphores. Data moves between devices by JAX's collectives and lax.ppermute only.
A program may use at most 64 MiB of HBM per device.

```python
import jax
import jax.numpy as jnp

C = 64
NX = 128
NY = 16
NZ = 64


def level_of(own_key, extent, shards, least, largest):
    loudness, own = 1.0, jax.random.fold_in(own_key, 6)
    for axis_at, shards_of in shards:
        heights = jnp.exp(jax.random.uniform(jax.random.fold_in(own, axis_at), (shards_of,), jnp.float32, least / len(shards), largest / len(shards)))
        loudness = loudness * jnp.repeat(heights, extent[axis_at] // shards_of).reshape([-1 if axis == axis_at else 1 for axis in range(len(extent))])
    return loudness


def bell_draw(own_key, extent, width, limit, cuts=(), dtype=jnp.bfloat16):
    level = level_of(own_key, extent, cuts, -0.22, 0.18) if cuts else 1.0
    entries = jax.random.normal(own_key, extent, jnp.float32) * width * level
    return jnp.minimum(jnp.maximum(entries, -limit), limit).astype(dtype)


def setup_inputs(seed: int = 0) -> dict:
    splits = jax.random.split(jax.random.key(seed), 5)
    return {
        "volume": bell_draw(splits[0], (C, NY, NZ, NX), 1.0, 6.0, ((0, 4), (1, 8), (2, 16))),
        "first_filters": bell_draw(splits[1], (C, 27 * C), (27 * C) ** -0.5, 0.15625, ((0, 4),)),
        "second_filters": bell_draw(splits[2], (C, 27 * C), (27 * C) ** -0.5, 0.15625, ((0, 4),)),
        "cotangent": bell_draw(splits[3], (C, NY, NZ, NX), 1.0, 6.0, ((0, 4), (1, 8), (2, 16))),
    }


OFFSETS = [(a, b, c) for a in range(3) for b in range(3) for c in range(3)]


def forward_conv(field, filters):
    channels = field.shape[0]
    voxels = field.shape[1] * field.shape[2] * field.shape[3]
    running = jnp.zeros((filters.shape[0], voxels), jnp.float32)
    for tap_index, (step_y, step_z, step_x) in enumerate(OFFSETS):
        shifted = jnp.roll(field, (1 - step_y, 1 - step_z, 1 - step_x), axis=(1, 2, 3)).reshape(channels, voxels)
        block = filters[:, tap_index * channels:(tap_index + 1) * channels]
        running = running + jnp.dot(block, shifted, preferred_element_type=jnp.float32)
    return running.reshape(field.shape)


def backward_conv(delta, filters):
    channels = delta.shape[0]
    voxels = delta.shape[1] * delta.shape[2] * delta.shape[3]
    running = jnp.zeros((channels, voxels), jnp.float32)
    for tap_index, (step_y, step_z, step_x) in enumerate(OFFSETS):
        shifted = jnp.roll(delta, (step_y - 1, step_z - 1, step_x - 1), axis=(1, 2, 3)).reshape(channels, voxels)
        block = filters[:, tap_index * channels:(tap_index + 1) * channels]
        running = running + jnp.dot(block.T, shifted, preferred_element_type=jnp.float32)
    return running.reshape(delta.shape)


def filter_gradient(delta, field):
    channels = field.shape[0]
    voxels = field.shape[1] * field.shape[2] * field.shape[3]
    flat_delta = delta.reshape(channels, voxels)
    blocks = []
    for step_y, step_z, step_x in OFFSETS:
        shifted = jnp.roll(field, (1 - step_y, 1 - step_z, 1 - step_x), axis=(1, 2, 3)).reshape(channels, voxels)
        blocks.append(jnp.dot(flat_delta, shifted.T, preferred_element_type=jnp.float32))
    factor = float(NX * NY * NZ) ** -0.5
    return jnp.concatenate(blocks, axis=1) * factor


def reference(volume, first_filters, second_filters, cotangent):
    first_pre = forward_conv(volume, first_filters)
    first_act = jax.nn.softplus(first_pre).astype(jnp.bfloat16)
    second_pre = forward_conv(first_act, second_filters)
    result = jax.nn.softplus(second_pre).astype(jnp.bfloat16)
    second_delta = (cotangent.astype(jnp.float32) * jax.nn.sigmoid(second_pre)).astype(jnp.bfloat16)
    second_grad = filter_gradient(second_delta, first_act)
    first_back = backward_conv(second_delta, second_filters)
    first_delta = (first_back * jax.nn.sigmoid(first_pre)).astype(jnp.bfloat16)
    first_grad = filter_gradient(first_delta, volume)
    grad_input = backward_conv(first_delta, first_filters).astype(jnp.bfloat16)
    return result, grad_input, first_grad, second_grad
```

```python
import jax
import jax.numpy as jnp
from jax import lax
from jax.experimental import pallas as pl
from jax.experimental.pallas import tpu as pltpu
from jax.sharding import PartitionSpec as P

BF = jnp.bfloat16
F32 = jnp.float32
C = 64
Y = 16
SY = 8
SZ = 16
FILT = 4
ZB = 4
XB = 4
RIM = 4
XW = XB + 2 * RIM
HALF = 2048
GRADS = 2 * HALF
PIECE = GRADS // 8
COLUMNS = 27 * C
PARAMS = pltpu.CompilerParams(vmem_limit_bytes=48 * 1024 * 1024)


def lanes_of(shape):
    return lax.broadcasted_iota(jnp.int32, shape, len(shape) - 1)


def turned(x, shift):
    return pltpu.roll(x, shift % x.shape[-1], x.ndim - 1)


def call(kernel, out_shape, scratch, *args):
    return pl.pallas_call(
        kernel, out_shape=out_shape, scratch_shapes=scratch, compiler_params=PARAMS
    )(*args)


def pack_kernel(volume_ref, cotangent_ref, out_ref, held):
    held[0:128, :] = volume_ref[...].astype(F32)
    held[128:256, :] = cotangent_ref[...].astype(F32)
    rows = [held[pl.ds(yz, 32, stride=8), :] for yz in range(8)]
    slot = lanes_of((32, 128)) // 16
    for k in range(SY * FILT):
        total = turned(rows[0], RIM - XB * k)
        for yz in range(1, 8):
            total = jnp.where(slot == yz, turned(rows[yz], 16 * yz + RIM - XB * k), total)
        out_ref[k] = total.astype(BF)


def unpack_kernel(in_ref, out_ref, held):
    for sy in range(SY):
        block = jnp.concatenate(
            [in_ref[sy * FILT + f, 16 * vc : 16 * vc + 16, :] for vc in range(2) for f in range(FILT)],
            axis=0,
        )
        flipped = jnp.transpose(block.astype(F32))
        for yy in range(2):
            for z in range(ZB):
                first = (yy * ZB + z) * 16
                held[pl.ds(z * XW * Y + 2 * sy + yy, XW, stride=Y), :] = flipped[first : first + XW, :]
    out_ref[...] = held[...].astype(BF)


def y_taps(x):
    cells = x.shape[0] // Y
    split = x.reshape(cells, Y, 128)
    before = pltpu.roll(split, 1, 1).reshape(x.shape)
    after = pltpu.roll(split, Y - 1, 1).reshape(x.shape)
    return before, after


def store_taps(ref, z, x):
    before, after = y_taps(x)
    low = lanes_of(x.shape) < C
    ref[z, :, 0:128] = jnp.where(low, before, x).astype(BF)
    ref[z, :, 128:256] = after.astype(BF)


def softplus(x):
    return jnp.maximum(x, 0.0) + jnp.log1p(jnp.exp(-jnp.abs(x)))


def sigmoid(x):
    e = jnp.exp(-jnp.abs(x))
    return jnp.where(x >= 0, 1.0, e) / (1.0 + e)


def tap_column(a, b, c):
    return (9 * a + 3 * b + c) * C


def fill_forward(ref, filters_ref):
    ref[...] = jnp.zeros_like(ref)
    for b in range(3):
        for a in range(3):
            for at, c in ((0, 0), (1, 1), (2, 2), (3, 2)):
                first = tap_column(a, b, c)
                ref[at * C : at * C + C, b * 256 + a * C : b * 256 + a * C + C] = filters_ref[
                    :, first : first + C
                ]


def fill_backward(ref, filters_ref):
    ref[...] = jnp.zeros_like(ref)
    for b in range(3):
        for a in range(3):
            for at, c in ((0, 0), (1, 1), (2, 2), (3, 2)):
                first = tap_column(2 - a, 2 - b, 2 - c)
                ref[b * 256 + a * C : b * 256 + a * C + C, at * C : at * C + C] = filters_ref[
                    :, first : first + C
                ]


def convolved(taps_ref, weights, z, wide, transposed):
    rows = wide * Y
    planes = jnp.concatenate([taps_ref[z + b, 0:rows, :] for b in range(3)], axis=1)
    dims = (((1,), (1 if transposed else 0,)), ((), ()))
    sums = lax.dot_general(planes, weights, dims, preferred_element_type=F32)
    left, right = sums[:, 0:128], sums[:, 128:256]
    swapped = turned(left, C)
    kept = rows - 2 * Y
    low = lanes_of((kept, 128)) < C
    return (
        jnp.where(
            low,
            left[0:kept] + swapped[Y : Y + kept],
            left[Y : Y + kept] + swapped[0:kept],
        )
        + right[2 * Y : 2 * Y + kept]
    )


def main_kernel(
    below_ref, own_ref, above_ref, first_ref, second_ref, out_ref,
    field, act, delta_2, delta_1, pre_1, cells_0, cells_1, cells_2, cells_3, weights, weights_t,
):
    slabs = (below_ref, own_ref, above_ref)
    plane = XW * Y

    def slab_rows(z, first, count):
        start = (z % ZB) * plane + first
        return slabs[z // ZB][start : start + count, :].astype(F32)

    fill_forward(weights.at[0], first_ref)
    fill_forward(weights.at[1], second_ref)
    fill_backward(weights_t.at[0], first_ref)
    fill_backward(weights_t.at[1], second_ref)
    for z in range(12):
        x = slab_rows(z, 0, plane)
        before, after = y_taps(x)
        low = lanes_of(x.shape) < C
        field[z, :, 0:128] = jnp.where(low, before, turned(x, C)).astype(BF)
        field[z, :, 128:256] = after.astype(BF)
    for z in range(10):
        pre = convolved(field, weights[0], z, 12, True)
        pre_1[z] = pre
        store_taps(act, z, softplus(pre).astype(BF).astype(F32))
    for z in range(8):
        pre = convolved(act, weights[1], z, 10, True)
        cotangent = slab_rows(z + 2, 2 * Y, 8 * Y)
        low = lanes_of(cotangent.shape) < C
        cotangent = jnp.where(low, turned(cotangent, C), cotangent)
        delta = (cotangent * sigmoid(pre)).astype(BF).astype(F32)
        store_taps(delta_2, z, delta)
        if 2 <= z < 6:
            own = slice((z - 2) * 64, (z - 1) * 64)
            cells_0[own, :] = softplus(pre[2 * Y : 6 * Y])
            cells_2[own, :] = delta[2 * Y : 6 * Y]
    for z in range(6):
        back = convolved(delta_2, weights_t[1], z, 8, False)
        delta = (back * sigmoid(pre_1[z + 2, 2 * Y : 8 * Y, :])).astype(BF).astype(F32)
        store_taps(delta_1, z, delta)
        if 1 <= z < 5:
            cells_3[(z - 1) * 64 : z * 64, :] = delta[Y : 5 * Y]
    for z in range(4):
        cells_1[z * 64 : z * 64 + 64, :] = convolved(delta_1, weights_t[0], z, 6, False)

    row = lax.broadcasted_iota(jnp.int32, (256, 256), 0)
    col = lax.broadcasted_iota(jnp.int32, (256, 256), 1)
    order = (row // 64) * 64 + (row % Y) * XB + (row // Y) % XB
    reorder = jnp.where(order == col, 1.0, 0.0).astype(BF)
    for at, cells in enumerate((cells_0, cells_1)):
        flat = jnp.transpose(cells[...])[0:C, :].astype(BF)
        out_ref[:, GRADS + at * 256 : GRADS + at * 256 + 256] = jnp.dot(
            flat, reorder, preferred_element_type=F32
        ).astype(BF)
    for base, cells, source, at in ((0, cells_3, field, 3), (HALF, cells_2, act, 2)):
        flat = jnp.transpose(cells[...])[0:C, :].astype(BF)
        for b in range(3):
            for c in range(3):
                near = jnp.concatenate(
                    [source[at + b + z, (at + c) * Y : (at + c + 4) * Y, :] for z in range(4)], axis=0
                )
                sums = jnp.dot(flat, near, preferred_element_type=F32).astype(BF)
                for a in range(3):
                    first = base + tap_column(a, b, c)
                    out_ref[:, first : first + C] = sums[:, a * C : a * C + C]
        out_ref[:, base + COLUMNS : base + HALF] = jnp.zeros((C, HALF - COLUMNS), BF)


def split_kernel(in_ref, out_ref):
    for q in range(8):
        total = in_ref[0, :, q * PIECE : (q + 1) * PIECE].astype(F32)
        for f in range(1, FILT):
            total = total + in_ref[f, :, q * PIECE : (q + 1) * PIECE].astype(F32)
        out_ref[q * 16 : q * 16 + 16, 0:PIECE] = total.astype(BF)
    for q in range(8):
        for f in range(FILT):
            out_ref[q * 16 : q * 16 + 16, PIECE + f * C : PIECE + f * C + C] = in_ref[
                f, :, GRADS + q * C : GRADS + q * C + C
            ]


def relay_kernel(in_ref, out_ref):
    total = jnp.sum(in_ref[:, 0:PIECE].astype(F32), axis=0, keepdims=True)
    out_ref[:, 0:PIECE] = jnp.broadcast_to(total, (128, PIECE)).astype(BF)
    row = lax.broadcasted_iota(jnp.int32, (256, 256), 0)
    col = lax.broadcasted_iota(jnp.int32, (256, 256), 1)
    order = ((row // 8) % SY) * 32 + (row // 64) * 8 + row % 8
    reorder = jnp.where(order == col, 1.0, 0.0).astype(BF)
    cells = jnp.dot(in_ref[:, PIECE : PIECE + 256], reorder, preferred_element_type=F32)
    slot = lanes_of((16, 128)) // 32
    for to in range(SY):
        for tile in range(2):
            total = None
            for at in range(4):
                sy = tile * 4 + at
                piece = cells[sy * 16 : sy * 16 + 16, (to // 4) * 128 : (to // 4) * 128 + 128]
                piece = turned(piece, (at - to % 4) * 32) if at != to % 4 else piece
                total = piece if total is None else jnp.where(slot == at, piece, total)
            first = PIECE + tile * 128
            out_ref[to * 16 : to * 16 + 16, first : first + 128] = total.astype(BF)


def finish_kernel(factor, in_ref, result_ref, grad_input_ref, first_ref, second_ref, held):
    for base, ref in ((0, first_ref), (4, second_ref)):
        for q in range(4):
            wide = min(PIECE, COLUMNS - q * PIECE)
            start = (base + q) * 16
            ref[:, q * PIECE : q * PIECE + wide] = in_ref[start : start + 16, 0:wide].astype(F32) * factor
    row = lax.broadcasted_iota(jnp.int32, (256, 256), 0)
    col = lax.broadcasted_iota(jnp.int32, (256, 256), 1)
    order = ((row // 4) % 2) * 128 + (row // 8) * 4 + row % 4
    reorder = jnp.where(order == col, 1.0, 0.0).astype(BF)
    cells = jnp.dot(in_ref[:, PIECE : PIECE + 256], reorder, preferred_element_type=F32)
    for at, ref in enumerate((result_ref, grad_input_ref)):
        for z in range(ZB):
            for yy in range(2):
                start = (at * ZB + z) * 16
                held[at, pl.ds(yy * ZB + z, 16, stride=8), :] = cells[
                    start : start + 16, yy * 128 : yy * 128 + 128
                ]
        ref[...] = held[at].astype(BF)


def body(volume, first_filters, second_filters, cotangent):
    shape = jax.ShapeDtypeStruct
    factor = float(SY * volume.shape[1] * SZ * volume.shape[2] * volume.shape[3]) ** -0.5
    with jax.named_scope("pack_windows"):
        packed = call(
            pack_kernel, shape((SY * FILT, 32, 128), BF), [pltpu.VMEM((256, 128), F32)],
            volume.reshape(128, 128), cotangent.reshape(128, 128),
        )
    with jax.named_scope("windows_exchange"):
        windows = lax.all_to_all(packed, ("sy", "filt"), 0, 0, tiled=True)
    with jax.named_scope("unpack_windows"):
        own = call(
            unpack_kernel, shape((ZB * XW * Y, 128), BF), [pltpu.VMEM((ZB * XW * Y, 128), F32)], windows
        )
    with jax.named_scope("z_rim_exchange"):
        below = lax.ppermute(own, "sz", [(i, (i + 1) % SZ) for i in range(SZ)])
        above = lax.ppermute(own, "sz", [((i + 1) % SZ, i) for i in range(SZ)])
    with jax.named_scope("filters_gather"):
        filters = lax.all_gather(jnp.concatenate([first_filters, second_filters], axis=1), "filt", axis=0, tiled=True)
        first, second = filters[:, :COLUMNS], filters[:, COLUMNS:]
    with jax.named_scope("layers"):
        partial = call(
            main_kernel,
            shape((C, GRADS + 512), BF),
            [
                pltpu.VMEM((12, 12 * Y, 256), BF),
                pltpu.VMEM((10, 10 * Y, 256), BF),
                pltpu.VMEM((8, 8 * Y, 256), BF),
                pltpu.VMEM((6, 6 * Y, 256), BF),
                pltpu.VMEM((10, 10 * Y, 128), F32),
                pltpu.VMEM((256, 128), F32),
                pltpu.VMEM((256, 128), F32),
                pltpu.VMEM((256, 128), F32),
                pltpu.VMEM((256, 128), F32),
                pltpu.VMEM((2, 256, 768), BF),
                pltpu.VMEM((2, 768, 256), BF),
            ],
            below, own, above, first, second,
        )
    with jax.named_scope("channel_exchange"):
        shares = lax.all_to_all(partial.reshape(FILT, 16, GRADS + 512), "filt", 0, 0, tiled=True)
    with jax.named_scope("split_shares"):
        rows = call(split_kernel, shape((128, PIECE + 256), BF), [], shares)
    with jax.named_scope("sum_exchange"):
        rows = lax.all_to_all(rows, ("sy", "sz"), 0, 0, tiled=True)
    with jax.named_scope("sum_and_relay"):
        rows = call(relay_kernel, shape((128, PIECE + 256), BF), [], rows)
    with jax.named_scope("spread_exchange"):
        rows = lax.all_to_all(rows, ("sy", "sz"), 0, 0, tiled=True)
    with jax.named_scope("finish"):
        result, grad_input, first_grad, second_grad = call(
            lambda *refs: finish_kernel(factor, *refs),
            (
                shape((128, 128), BF), shape((128, 128), BF),
                shape((16, COLUMNS), F32), shape((16, COLUMNS), F32),
            ),
            [pltpu.VMEM((2, 128, 128), F32)],
            rows,
        )
    return (result.reshape(volume.shape), grad_input.reshape(volume.shape), first_grad, second_grad)


def solution(mesh):
    return jax.shard_map(
        body,
        mesh=mesh,
        in_specs=(
            P("filt", "sy", "sz", None),
            P("filt", None),
            P("filt", None),
            P("filt", "sy", "sz", None),
        ),
        out_specs=(
            P("filt", "sy", "sz", None),
            P("filt", "sy", "sz", None),
            P("filt", None),
            P("filt", None),
        ),
        check_vma=False,
    )
```

```python
import jax
import jax.numpy as jnp
from jax import lax
from jax.experimental import pallas as pl
from jax.experimental.pallas import tpu as pltpu
from jax.sharding import PartitionSpec as P

BF = jnp.bfloat16
F32 = jnp.float32
C = 64
Y = 16
SY = 8
SZ = 16
FILT = 4
SYH = SY // 2
ZB = 4
XB = 8
RIM = 4
XW = XB + 2 * RIM
PLANE = XW * Y
BLOCKS = SYH * FILT
HALF = 2048
GRADS = 2 * HALF
QUARTER = GRADS // SYH
PIECE = QUARTER // 4
COLUMNS = 27 * C
PARAMS = pltpu.CompilerParams(vmem_limit_bytes=48 * 1024 * 1024)


def at_device(half, y, z, core):
    return (half * SYH + y) * SZ + z * 2 + core


PENCIL = ("sy", "sz")
HALVES, PAIRS, CORES = range(2), range(SZ // 4), range(2)
SAME_HALF = [[half * BLOCKS + i for i in range(BLOCKS)] for half in HALVES]
FOURS = [
    [at_device(half, y, 2 * pair + odd, core) for odd in HALVES for core in CORES]
    for half in HALVES for y in range(SYH) for pair in PAIRS
]
EIGHTS = [
    [at_device(half, y, 2 * pair + odd, core) for half in HALVES for pair in PAIRS]
    for y in range(SYH) for odd in HALVES for core in CORES
]
SIXTEENS = [
    [at_device(half, y, 2 * pair + odd, core) for y in range(SYH) for odd in HALVES for core in CORES]
    for half in HALVES for pair in PAIRS
]


def along_z(step):
    pairs = []
    for half in HALVES:
        for y in range(SYH):
            for z in range(SZ):
                to = (half * SZ + z + step) % (2 * SZ)
                pairs.append((half * SYH * SZ + y * SZ + z, (to // SZ) * SYH * SZ + y * SZ + to % SZ))
    return pairs


def lanes_of(shape):
    return lax.broadcasted_iota(jnp.int32, shape, len(shape) - 1)


def turned(x, shift):
    return pltpu.roll(x, shift % x.shape[-1], x.ndim - 1)


def call(kernel, out_shape, scratch, *args):
    return pl.pallas_call(
        kernel, out_shape=out_shape, scratch_shapes=scratch, compiler_params=PARAMS
    )(*args)


def pack_kernel(volume_ref, cotangent_ref, first_ref, second_ref, out_ref, filters_ref, held):
    held[0:128, :] = volume_ref[...].astype(F32)
    held[128:256, :] = cotangent_ref[...].astype(F32)
    rows = [held[pl.ds(yz, 32, stride=8), :] for yz in range(8)]
    slot = lanes_of((32, 128)) // 16
    for k in range(BLOCKS):
        total = turned(rows[0], RIM - XB * k)
        for yz in range(1, 8):
            total = jnp.where(slot == yz, turned(rows[yz], 16 * yz + RIM - XB * k), total)
        total = total.astype(BF)
        out_ref[k] = total
        out_ref[BLOCKS + k] = total
    for f in range(FILT):
        filters_ref[f, 0] = first_ref[...]
        filters_ref[f, 1] = second_ref[...]


def unpack_kernel(in_ref, out_ref, held):
    for sy in range(SY):
        block = jnp.concatenate(
            [in_ref[sy * FILT + f, 16 * vc : 16 * vc + 16, :] for vc in range(2) for f in range(FILT)],
            axis=0,
        )
        flipped = jnp.transpose(block.astype(F32))
        for yy in range(2):
            for z in range(ZB):
                first = (yy * ZB + z) * XW
                held[pl.ds(z * PLANE + 2 * sy + yy, XW, stride=Y), :] = flipped[first : first + XW, :]
    out_ref[...] = held[...].astype(BF)


def y_taps(x):
    cells = x.shape[0] // Y
    split = x.reshape(cells, Y, 128)
    before = pltpu.roll(split, 1, 1).reshape(x.shape)
    after = pltpu.roll(split, Y - 1, 1).reshape(x.shape)
    return before, after


def store_taps(ref, z, x):
    before, after = y_taps(x)
    low = lanes_of(x.shape) < C
    ref[z, :, 0:128] = jnp.where(low, before, x).astype(BF)
    ref[z, :, 128:256] = after.astype(BF)


def softplus(x):
    return jnp.maximum(x, 0.0) + jnp.log1p(jnp.exp(-jnp.abs(x)))


def sigmoid(x):
    e = jnp.exp(-jnp.abs(x))
    return jnp.where(x >= 0, 1.0, e) / (1.0 + e)


def tap_column(a, b, c):
    return (9 * a + 3 * b + c) * C


def fill_forward(ref, filters_ref, layer):
    ref[...] = jnp.zeros_like(ref)
    for b in range(3):
        for a in range(3):
            for at, c in ((0, 0), (1, 1), (2, 2), (3, 2)):
                first = tap_column(a, b, c)
                for f in range(FILT):
                    row = at * C + f * 16
                    ref[row : row + 16, b * 256 + a * C : b * 256 + a * C + C] = filters_ref[
                        f, layer, :, first : first + C
                    ]


def fill_backward(ref, filters_ref, layer):
    ref[...] = jnp.zeros_like(ref)
    for b in range(3):
        for a in range(3):
            for at, c in ((0, 0), (1, 1), (2, 2), (3, 2)):
                first = tap_column(2 - a, 2 - b, 2 - c)
                for f in range(FILT):
                    row = b * 256 + a * C + f * 16
                    ref[row : row + 16, at * C : at * C + C] = filters_ref[
                        f, layer, :, first : first + C
                    ]


def convolved(taps_ref, weights, z, wide, transposed):
    rows = wide * Y
    planes = jnp.concatenate([taps_ref[z + b, 0:rows, :] for b in range(3)], axis=1)
    dims = (((1,), (1 if transposed else 0,)), ((), ()))
    sums = lax.dot_general(planes, weights, dims, preferred_element_type=F32)
    left, right = sums[:, 0:128], sums[:, 128:256]
    swapped = turned(left, C)
    kept = rows - 2 * Y
    low = lanes_of((kept, 128)) < C
    return (
        jnp.where(
            low,
            left[0:kept] + swapped[Y : Y + kept],
            left[Y : Y + kept] + swapped[0:kept],
        )
        + right[2 * Y : 2 * Y + kept]
    )


def main_kernel(
    below_ref, own_ref, above_ref, filters_ref, out_ref,
    field, act, delta_2, delta_1, pre_1, cells_0, cells_1, cells_2, cells_3, weights, weights_t,
):
    half = lax.axis_index("sy") // SYH
    slabs = (below_ref, own_ref, above_ref)

    def slab_rows(z, first, count):
        start = (z % ZB) * PLANE + first
        return slabs[z // ZB][start : start + count, :].astype(F32)

    for layer in range(2):
        fill_forward(weights.at[layer], filters_ref, layer)
        fill_backward(weights_t.at[layer], filters_ref, layer)
    for z in range(12):
        x = slab_rows(z, 0, PLANE)
        before, after = y_taps(x)
        low = lanes_of(x.shape) < C
        field[z, :, 0:128] = jnp.where(low, before, turned(x, C)).astype(BF)
        field[z, :, 128:256] = after.astype(BF)
    for z in range(10):
        pre = convolved(field, weights[0], z, XW, True)
        pre_1[z] = pre
        store_taps(act, z, softplus(pre).astype(BF).astype(F32))
    for z in range(8):
        pre = convolved(act, weights[1], z, XW - 2, True)
        cotangent = slab_rows(z + 2, 2 * Y, (XW - 4) * Y)
        low = lanes_of(cotangent.shape) < C
        cotangent = jnp.where(low, turned(cotangent, C), cotangent)
        delta = (cotangent * sigmoid(pre)).astype(BF).astype(F32)
        store_taps(delta_2, z, delta)
        if 2 <= z < 6:
            cells_0[z - 2] = softplus(pre[2 * Y : (2 + XB) * Y])
            cells_2[z - 2] = delta[2 * Y : (2 + XB) * Y]
    for z in range(6):
        back = convolved(delta_2, weights_t[1], z, XW - 4, False)
        delta = (back * sigmoid(pre_1[z + 2, 2 * Y : (XW - 4) * Y, :])).astype(BF).astype(F32)
        store_taps(delta_1, z, delta)
        if 1 <= z < 5:
            cells_3[z - 1] = delta[Y : (1 + XB) * Y]
    for z in range(4):
        cells_1[z] = convolved(delta_1, weights_t[0], z, XW - 6, False)

    count = ZB * XB * Y
    row = lax.broadcasted_iota(jnp.int32, (count, count // 2), 0)
    col = lax.broadcasted_iota(jnp.int32, (count, count // 2), 1)
    y = row % Y - half * (Y // 2)
    order = (y // 2) * 64 + (row // (XB * Y)) * 16 + (y % 2) * XB + (row // Y) % XB
    inside = (y >= 0) & (y < Y // 2)
    reorder = jnp.where(inside & (order == col), 1.0, 0.0).astype(BF)
    for at, cells in enumerate((cells_0, cells_1)):
        flat = jnp.transpose(cells[...].reshape(count, 128))[0:C, :].astype(BF)
        flat = jnp.dot(flat, reorder, preferred_element_type=F32).astype(BF)
        for to in range(SYH):
            first = QUARTER + at * 64
            out_ref[to, :, first : first + 64] = flat[:, to * 64 : to * 64 + 64]
    for base, cells, source, at in ((0, cells_3, field, 3), (HALF, cells_2, act, 2)):
        own = pl.ds(pl.multiple_of(half * 64, 64), 64)
        flat = jnp.transpose(cells[:, own, :].reshape(256, 128))[0:C, :].astype(BF)
        for b in range(3):
            for c in range(3):
                near = pl.ds(pl.multiple_of((at + c) * Y + half * 64, 16), 64)
                near = jnp.concatenate([source[at + b + z, near, :] for z in range(4)], axis=0)
                sums = jnp.dot(flat, near, preferred_element_type=F32).astype(BF)
                for a in range(3):
                    first = base + tap_column(a, b, c)
                    to, first = first // QUARTER, first % QUARTER
                    out_ref[to, :, first : first + C] = sums[:, a * C : a * C + C]
        out_ref[(base + COLUMNS) // QUARTER, :, (base + COLUMNS) % QUARTER : QUARTER] = jnp.zeros(
            (C, HALF - COLUMNS), BF
        )


def split_kernel(in_ref, out_ref, result_ref, grad_input_ref, held):
    for to in range(4):
        lanes = slice(to * PIECE, (to + 1) * PIECE)
        total = in_ref[0, :, lanes].astype(F32)
        for k in range(1, BLOCKS):
            total = total + in_ref[k, :, lanes].astype(F32)
        out_ref[to] = total.astype(BF)
    blocks = [in_ref[k, :, QUARTER : QUARTER + 128].astype(F32) for k in range(BLOCKS)]
    slot = lanes_of((16, 128)) // XB
    for at, ref in enumerate((result_ref, grad_input_ref)):
        for z in range(ZB):
            for yy in range(2):
                first = at * 64 + z * 16 + yy * XB
                total = turned(blocks[0], -first)
                for k in range(1, BLOCKS):
                    total = jnp.where(slot == k, turned(blocks[k], k * XB - first), total)
                held[at, pl.ds(yy * ZB + z, 16, stride=8), :] = total
        ref[...] = held[at].astype(BF)


def sum_kernel(in_ref, out_ref):
    total = in_ref[0].astype(F32)
    for k in range(1, in_ref.shape[0]):
        total = total + in_ref[k].astype(F32)
    total = total.astype(BF)
    for k in range(out_ref.shape[0]):
        out_ref[k] = total


def finish_kernel(factor, in_ref, first_ref, second_ref):
    for base, ref in ((0, first_ref), (8, second_ref)):
        for k in range(7):
            wide = min(PIECE, COLUMNS - k * PIECE)
            ref[:, k * PIECE : k * PIECE + wide] = in_ref[base + k, :, 0:wide].astype(F32) * factor


def body(volume, first_filters, second_filters, cotangent):
    shape = jax.ShapeDtypeStruct
    factor = float(SY * volume.shape[1] * SZ * volume.shape[2] * volume.shape[3]) ** -0.5
    with jax.named_scope("pack_windows"):
        packed, filters = call(
            pack_kernel,
            (shape((SY * FILT, 32, 128), BF), shape((FILT, 2, 16, COLUMNS), BF)),
            [pltpu.VMEM((256, 128), F32)],
            volume.reshape(128, 128), cotangent.reshape(128, 128), first_filters, second_filters,
        )
    with jax.named_scope("windows_exchange"):
        windows = lax.all_to_all(packed, ("sy", "filt"), 0, 0, tiled=True)
    with jax.named_scope("unpack_windows"):
        own = call(unpack_kernel, shape((ZB * PLANE, 128), BF), [pltpu.VMEM((ZB * PLANE, 128), F32)], windows)
    with jax.named_scope("z_rim_exchange"):
        below = lax.ppermute(own, PENCIL, along_z(1))
        above = lax.ppermute(own, PENCIL, along_z(-1))
    with jax.named_scope("filters_exchange"):
        filters, own = lax.optimization_barrier((filters, own))
        filters = lax.all_to_all(filters, "filt", 0, 0, tiled=True)
    with jax.named_scope("layers"):
        partial = call(
            main_kernel,
            shape((SYH, C, QUARTER + 128), BF),
            [
                pltpu.VMEM((12, XW * Y, 256), BF),
                pltpu.VMEM((10, (XW - 2) * Y, 256), BF),
                pltpu.VMEM((8, (XW - 4) * Y, 256), BF),
                pltpu.VMEM((6, (XW - 6) * Y, 256), BF),
                pltpu.VMEM((10, (XW - 2) * Y, 128), F32),
                pltpu.VMEM((ZB, XB * Y, 128), F32),
                pltpu.VMEM((ZB, XB * Y, 128), F32),
                pltpu.VMEM((ZB, XB * Y, 128), F32),
                pltpu.VMEM((ZB, XB * Y, 128), F32),
                pltpu.VMEM((2, 256, 768), BF),
                pltpu.VMEM((2, 768, 256), BF),
            ],
            below, own, above, filters,
        )
    with jax.named_scope("blocks_exchange"):
        shares = partial.reshape(BLOCKS, 16, QUARTER + 128)
        shares = lax.all_to_all(shares, ("sy", "filt"), 0, 0, tiled=True, axis_index_groups=SAME_HALF)
    with jax.named_scope("split_shares"):
        pieces, result, grad_input = call(
            split_kernel,
            (shape((4, 16, PIECE), BF), shape((128, 128), BF), shape((128, 128), BF)),
            [pltpu.VMEM((2, 128, 128), F32)],
            shares,
        )
    with jax.named_scope("near_sum_exchange"):
        pieces = lax.all_to_all(pieces, PENCIL, 0, 0, tiled=True, axis_index_groups=FOURS)
        pieces = call(sum_kernel, shape((8, 16, PIECE), BF), [], pieces)
    with jax.named_scope("far_sum_exchange"):
        pieces = lax.all_to_all(pieces, PENCIL, 0, 0, tiled=True, axis_index_groups=EIGHTS)
        pieces = call(sum_kernel, shape((16, 16, PIECE), BF), [], pieces)
    with jax.named_scope("spread_exchange"):
        pieces = lax.all_to_all(pieces, PENCIL, 0, 0, tiled=True, axis_index_groups=SIXTEENS)
    with jax.named_scope("finish"):
        first_grad, second_grad = call(
            lambda *refs: finish_kernel(factor, *refs),
            (shape((16, COLUMNS), F32), shape((16, COLUMNS), F32)),
            [],
            pieces,
        )
    return (result.reshape(volume.shape), grad_input.reshape(volume.shape), first_grad, second_grad)


def solution(mesh):
    return jax.shard_map(
        body,
        mesh=mesh,
        in_specs=(
            P("filt", "sy", "sz", None),
            P("filt", None),
            P("filt", None),
            P("filt", "sy", "sz", None),
        ),
        out_specs=(
            P("filt", "sy", "sz", None),
            P("filt", "sy", "sz", None),
            P("filt", None),
            P("filt", None),
        ),
        check_vma=False,
    )
```

```python
import jax
import jax.numpy as jnp
from jax import lax
from jax.experimental import pallas as pl
from jax.experimental.pallas import tpu as pltpu
from jax.sharding import PartitionSpec as P

BF = jnp.bfloat16
F32 = jnp.float32
C = 64
Y = 16
SY = 8
SZ = 16
FILT = 4
SYH = SY // 2
ZB = 4
XB = 8
RIM = 4
XW = XB + 2 * RIM
PLANE = XW * Y
BLOCKS = SYH * FILT
HALF = 28 * C
GRADS = 2 * HALF
QUARTER = GRADS // SYH
PIECE = 256
TILES = HALF // (SYH // 2) // 128
COLUMNS = 27 * C
PARAMS = pltpu.CompilerParams(vmem_limit_bytes=48 * 1024 * 1024)


def at_device(half, y, z, core):
    return (half * SYH + y) * SZ + z * 2 + core


PENCIL = ("sy", "sz")
HALVES, PAIRS, CORES = range(2), range(SZ // 4), range(2)
SAME_HALF = [[half * BLOCKS + i for i in range(BLOCKS)] for half in HALVES]
FOURS = [
    [at_device(half, y, 2 * pair + odd, core) for odd in HALVES for core in CORES]
    for half in HALVES for y in range(SYH) for pair in PAIRS
]
EIGHTS = [
    [at_device(half, y, 2 * pair + odd, core) for half in HALVES for pair in PAIRS]
    for y in range(SYH) for odd in HALVES for core in CORES
]
SIXTEENS = [
    [at_device(half, y, 2 * pair + odd, core) for y in range(SYH) for odd in HALVES for core in CORES]
    for half in HALVES for pair in PAIRS
]


def along_z(step):
    pairs = []
    for half in HALVES:
        for y in range(SYH):
            for z in range(SZ):
                to = (half * SZ + z + step) % (2 * SZ)
                pairs.append((half * SYH * SZ + y * SZ + z, (to // SZ) * SYH * SZ + y * SZ + to % SZ))
    return pairs


def lanes_of(shape):
    return lax.broadcasted_iota(jnp.int32, shape, len(shape) - 1)


def turned(x, shift):
    return pltpu.roll(x, shift % x.shape[-1], x.ndim - 1)


def call(kernel, out_shape, scratch, *args):
    return pl.pallas_call(
        kernel, out_shape=out_shape, scratch_shapes=scratch, compiler_params=PARAMS
    )(*args)


def pack_kernel(near_ref, far_ref, first_ref, second_ref, out_ref, held, filters):
    filters[...] = jnp.zeros_like(filters)
    filters[:, 0:COLUMNS] = first_ref[...]
    filters[:, HALF : HALF + COLUMNS] = second_ref[...]
    share = lax.axis_index("sy") % SYH
    for tile in range(TILES):
        first = pl.multiple_of((share * TILES + tile) * 128, 128)
        columns = filters[:, pl.ds(first, 128)]
        for k in range(BLOCKS):
            out_ref[k, 64 + 16 * tile : 80 + 16 * tile, :] = columns
    lower = lax.axis_index("sy") < SYH
    near, far = near_ref[...].astype(F32), far_ref[...].astype(F32)
    held[0:256, :] = jnp.where(lower, near, far)
    held[256:512, :] = jnp.where(lower, far, near)
    rows = [held[pl.ds(yz, 64, stride=8), :] for yz in range(8)]
    slot = lanes_of((64, 128)) // 16
    for k in range(BLOCKS):
        total = turned(rows[0], RIM - XB * k)
        for yz in range(1, 8):
            total = jnp.where(slot == yz, turned(rows[yz], 16 * yz + RIM - XB * k), total)
        out_ref[k, 0:64, :] = total.astype(BF)


def unpack_kernel(in_ref, out_ref, held):
    for sy in range(SY):
        top = (sy // SYH) * 32
        block = jnp.concatenate(
            [
                in_ref[(sy % SYH) * FILT + f, top + 16 * vc : top + 16 * vc + 16, :]
                for vc in range(2) for f in range(FILT)
            ],
            axis=0,
        )
        flipped = jnp.transpose(block.astype(F32))
        for yy in range(2):
            for z in range(ZB):
                first = (yy * ZB + z) * XW
                held[pl.ds(z * PLANE + 2 * sy + yy, XW, stride=Y), :] = flipped[first : first + XW, :]
    out_ref[...] = held[...].astype(BF)


def y_taps(x):
    cells = x.shape[0] // Y
    split = x.reshape(cells, Y, 128)
    before = pltpu.roll(split, 1, 1).reshape(x.shape)
    after = pltpu.roll(split, Y - 1, 1).reshape(x.shape)
    return before, after


def store_taps(ref, z, x):
    before, after = y_taps(x)
    low = lanes_of(x.shape) < C
    ref[z, :, 0:128] = jnp.where(low, before, x).astype(BF)
    ref[z, :, 128:256] = after.astype(BF)


def softplus(x):
    return jnp.maximum(x, 0.0) + jnp.log1p(jnp.exp(-jnp.abs(x)))


def sigmoid(x):
    e = jnp.exp(-jnp.abs(x))
    return jnp.where(x >= 0, 1.0, e) / (1.0 + e)


def tap_column(a, b, c):
    return (9 * a + 3 * b + c) * C


def filter_block(windows_ref, layer, f, a, b, c):
    column = layer * HALF + tap_column(a, b, c)
    tile = column // 128
    top = 64 + 16 * (tile % TILES)
    return windows_ref[(tile // TILES) * FILT + f, top : top + 16, column % 128 : column % 128 + C]


def fill_forward(ref, windows_ref, layer):
    ref[...] = jnp.zeros_like(ref)
    for b in range(3):
        for a in range(3):
            for at, c in ((0, 0), (1, 1), (2, 2), (3, 2)):
                for f in range(FILT):
                    row = at * C + f * 16
                    ref[row : row + 16, b * 256 + a * C : b * 256 + a * C + C] = filter_block(
                        windows_ref, layer, f, a, b, c
                    )


def fill_backward(ref, windows_ref, layer):
    ref[...] = jnp.zeros_like(ref)
    for b in range(3):
        for a in range(3):
            for at, c in ((0, 0), (1, 1), (2, 2), (3, 2)):
                for f in range(FILT):
                    row = b * 256 + a * C + f * 16
                    ref[row : row + 16, at * C : at * C + C] = filter_block(
                        windows_ref, layer, f, 2 - a, 2 - b, 2 - c
                    )


def convolved(taps_ref, weights, z, wide, transposed):
    rows = wide * Y
    planes = jnp.concatenate([taps_ref[z + b, 0:rows, :] for b in range(3)], axis=1)
    dims = (((1,), (1 if transposed else 0,)), ((), ()))
    sums = lax.dot_general(planes, weights, dims, preferred_element_type=F32)
    left, right = sums[:, 0:128], sums[:, 128:256]
    swapped = turned(left, C)
    kept = rows - 2 * Y
    low = lanes_of((kept, 128)) < C
    return (
        jnp.where(
            low,
            left[0:kept] + swapped[Y : Y + kept],
            left[Y : Y + kept] + swapped[0:kept],
        )
        + right[2 * Y : 2 * Y + kept]
    )


def main_kernel(
    below_ref, own_ref, above_ref, windows_ref, out_ref,
    field, act, delta_2, delta_1, pre_1, cells_0, cells_1, cells_2, cells_3, weights, weights_t,
):
    half = lax.axis_index("sy") // SYH
    slabs = (below_ref, own_ref, above_ref)

    def slab_rows(z, first, count):
        start = (z % ZB) * PLANE + first
        return slabs[z // ZB][start : start + count, :].astype(F32)

    for layer in range(2):
        fill_forward(weights.at[layer], windows_ref, layer)
        fill_backward(weights_t.at[layer], windows_ref, layer)
    for z in range(12):
        x = slab_rows(z, 0, PLANE)
        before, after = y_taps(x)
        low = lanes_of(x.shape) < C
        field[z, :, 0:128] = jnp.where(low, before, turned(x, C)).astype(BF)
        field[z, :, 128:256] = after.astype(BF)
    for z in range(10):
        pre = convolved(field, weights[0], z, XW, True)
        pre_1[z] = pre
        store_taps(act, z, softplus(pre).astype(BF).astype(F32))
    for z in range(8):
        pre = convolved(act, weights[1], z, XW - 2, True)
        cotangent = slab_rows(z + 2, 2 * Y, (XW - 4) * Y)
        low = lanes_of(cotangent.shape) < C
        cotangent = jnp.where(low, turned(cotangent, C), cotangent)
        delta = (cotangent * sigmoid(pre)).astype(BF).astype(F32)
        store_taps(delta_2, z, delta)
        if 2 <= z < 6:
            cells_0[z - 2] = softplus(pre[2 * Y : (2 + XB) * Y])
            cells_2[z - 2] = delta[2 * Y : (2 + XB) * Y]
    for z in range(6):
        back = convolved(delta_2, weights_t[1], z, XW - 4, False)
        delta = (back * sigmoid(pre_1[z + 2, 2 * Y : (XW - 4) * Y, :])).astype(BF).astype(F32)
        store_taps(delta_1, z, delta)
        if 1 <= z < 5:
            cells_3[z - 1] = delta[Y : (1 + XB) * Y]
    for z in range(4):
        cells_1[z] = convolved(delta_1, weights_t[0], z, XW - 6, False)

    count = ZB * XB * Y
    row = lax.broadcasted_iota(jnp.int32, (count, count // 2), 0)
    col = lax.broadcasted_iota(jnp.int32, (count, count // 2), 1)
    y = row % Y - half * (Y // 2)
    order = (y // 2) * 64 + (row // (XB * Y)) * 16 + (y % 2) * XB + (row // Y) % XB
    inside = (y >= 0) & (y < Y // 2)
    reorder = jnp.where(inside & (order == col), 1.0, 0.0).astype(BF)
    for at, cells in enumerate((cells_0, cells_1)):
        flat = jnp.transpose(cells[...].reshape(count, 128))[0:C, :].astype(BF)
        flat = jnp.dot(flat, reorder, preferred_element_type=F32).astype(BF)
        for to in range(SYH):
            first = QUARTER + at * 64
            out_ref[to, :, first : first + 64] = flat[:, to * 64 : to * 64 + 64]
    for base, cells, source, at in ((0, cells_3, field, 3), (HALF, cells_2, act, 2)):
        own = pl.ds(pl.multiple_of(half * 64, 64), 64)
        flat = jnp.transpose(cells[:, own, :].reshape(256, 128))[0:C, :].astype(BF)
        for b in range(3):
            for c in range(3):
                near = pl.ds(pl.multiple_of((at + c) * Y + half * 64, 16), 64)
                near = jnp.concatenate([source[at + b + z, near, :] for z in range(4)], axis=0)
                sums = jnp.dot(flat, near, preferred_element_type=F32).astype(BF)
                for a in range(3):
                    first = base + tap_column(a, b, c)
                    to, first = first // QUARTER, first % QUARTER
                    out_ref[to, :, first : first + C] = sums[:, a * C : a * C + C]
        out_ref[(base + COLUMNS) // QUARTER, :, (base + COLUMNS) % QUARTER : QUARTER] = jnp.zeros(
            (C, HALF - COLUMNS), BF
        )


def split_kernel(in_ref, out_ref):
    for to in range(4):
        wide = min(PIECE, QUARTER - to * PIECE)
        lanes = slice(to * PIECE, to * PIECE + wide)
        total = in_ref[0, :, lanes].astype(F32)
        for k in range(1, BLOCKS):
            total = total + in_ref[k, :, lanes].astype(F32)
        out_ref[to, :, 0:wide] = total.astype(BF)
        if wide < PIECE:
            out_ref[to, :, wide:PIECE] = jnp.zeros((16, PIECE - wide), BF)


def outputs_kernel(in_ref, result_ref, grad_input_ref, held):
    blocks = [in_ref[k, :, QUARTER : QUARTER + 128].astype(F32) for k in range(BLOCKS)]
    slot = lanes_of((16, 128)) // XB
    for at, ref in enumerate((result_ref, grad_input_ref)):
        for z in range(ZB):
            for yy in range(2):
                first = at * 64 + z * 16 + yy * XB
                total = turned(blocks[0], -first)
                for k in range(1, BLOCKS):
                    total = jnp.where(slot == k, turned(blocks[k], k * XB - first), total)
                held[at, pl.ds(yy * ZB + z, 16, stride=8), :] = total
        ref[...] = held[at].astype(BF)


def sum_kernel(in_ref, out_ref):
    total = in_ref[0].astype(F32)
    for k in range(1, in_ref.shape[0]):
        total = total + in_ref[k].astype(F32)
    total = total.astype(BF)
    for k in range(out_ref.shape[0]):
        out_ref[k] = total


def finish_kernel(factor, in_ref, first_ref, second_ref):
    for base, ref in ((0, first_ref), (8, second_ref)):
        for k in range(8):
            first = (k // 4) * QUARTER + (k % 4) * PIECE
            wide = min(PIECE, QUARTER - (k % 4) * PIECE, COLUMNS - first)
            ref[:, first : first + wide] = in_ref[base + k, :, 0:wide].astype(F32) * factor


def body(volume, first_filters, second_filters, cotangent):
    shape = jax.ShapeDtypeStruct
    factor = float(SY * volume.shape[1] * SZ * volume.shape[2] * volume.shape[3]) ** -0.5
    with jax.named_scope("halves_exchange"):
        near = jnp.concatenate([volume.reshape(128, 128), cotangent.reshape(128, 128)], axis=0)
        far = lax.ppermute(near, "sy", [(i, (i + SYH) % SY) for i in range(SY)])
    with jax.named_scope("pack_windows"):
        packed = call(
            pack_kernel,
            shape((BLOCKS, 64 + 16 * TILES, 128), BF),
            [pltpu.VMEM((512, 128), F32), pltpu.VMEM((16, 2 * HALF), BF)],
            near, far, first_filters, second_filters,
        )
    with jax.named_scope("windows_exchange"):
        windows = lax.all_to_all(packed, ("sy", "filt"), 0, 0, tiled=True, axis_index_groups=SAME_HALF)
    with jax.named_scope("unpack_windows"):
        own = call(unpack_kernel, shape((ZB * PLANE, 128), BF), [pltpu.VMEM((ZB * PLANE, 128), F32)], windows)
    with jax.named_scope("z_rim_exchange"):
        below = lax.ppermute(own, PENCIL, along_z(1))
        above = lax.ppermute(own, PENCIL, along_z(-1))
    with jax.named_scope("layers"):
        partial = call(
            main_kernel,
            shape((SYH, C, QUARTER + 128), BF),
            [
                pltpu.VMEM((12, XW * Y, 256), BF),
                pltpu.VMEM((10, (XW - 2) * Y, 256), BF),
                pltpu.VMEM((8, (XW - 4) * Y, 256), BF),
                pltpu.VMEM((6, (XW - 6) * Y, 256), BF),
                pltpu.VMEM((10, (XW - 2) * Y, 128), F32),
                pltpu.VMEM((ZB, XB * Y, 128), F32),
                pltpu.VMEM((ZB, XB * Y, 128), F32),
                pltpu.VMEM((ZB, XB * Y, 128), F32),
                pltpu.VMEM((ZB, XB * Y, 128), F32),
                pltpu.VMEM((2, 256, 768), BF),
                pltpu.VMEM((2, 768, 256), BF),
            ],
            below, own, above, windows,
        )
    with jax.named_scope("blocks_exchange"):
        shares = partial.reshape(BLOCKS, 16, QUARTER + 128)
        shares = lax.all_to_all(shares, ("sy", "filt"), 0, 0, tiled=True, axis_index_groups=SAME_HALF)
    with jax.named_scope("split_shares"):
        pieces = call(split_kernel, shape((4, 16, PIECE), BF), [], shares)
    with jax.named_scope("place_outputs"):
        result, grad_input = call(
            outputs_kernel,
            (shape((128, 128), BF), shape((128, 128), BF)),
            [pltpu.VMEM((2, 128, 128), F32)],
            shares,
        )
    with jax.named_scope("near_sum_exchange"):
        pieces = lax.all_to_all(pieces, PENCIL, 0, 0, tiled=True, axis_index_groups=FOURS)
        pieces = call(sum_kernel, shape((8, 16, PIECE), BF), [], pieces)
    with jax.named_scope("far_sum_exchange"):
        pieces = lax.all_to_all(pieces, PENCIL, 0, 0, tiled=True, axis_index_groups=EIGHTS)
        pieces = call(sum_kernel, shape((16, 16, PIECE), BF), [], pieces)
    with jax.named_scope("spread_exchange"):
        pieces = lax.all_to_all(pieces, PENCIL, 0, 0, tiled=True, axis_index_groups=SIXTEENS)
    with jax.named_scope("finish"):
        first_grad, second_grad = call(
            lambda *refs: finish_kernel(factor, *refs),
            (shape((16, COLUMNS), F32), shape((16, COLUMNS), F32)),
            [],
            pieces,
        )
    return (result.reshape(volume.shape), grad_input.reshape(volume.shape), first_grad, second_grad)


def solution(mesh):
    return jax.shard_map(
        body,
        mesh=mesh,
        in_specs=(
            P("filt", "sy", "sz", None),
            P("filt", None),
            P("filt", None),
            P("filt", "sy", "sz", None),
        ),
        out_specs=(
            P("filt", "sy", "sz", None),
            P("filt", "sy", "sz", None),
            P("filt", None),
            P("filt", None),
        ),
        check_vma=False,
    )
```

```python
import jax
import jax.numpy as jnp
from jax import lax
from jax.experimental import pallas as pl
from jax.experimental.pallas import tpu as pltpu
from jax.sharding import PartitionSpec as P

BF = jnp.bfloat16
F32 = jnp.float32
C = 64
Y = 16
SY = 8
SZ = 16
FILT = 4
SYH = SY // 2
ZB = 4
XB = 8
RIM = 4
XW = XB + 2 * RIM
PLANE = XW * Y
BLOCKS = SYH * FILT
HALF = 28 * C
GRADS = 2 * HALF
QUARTER = GRADS // SYH
PIECE = 256
TILES = HALF // (SYH // 2) // 128
COLUMNS = 27 * C
PARAMS = pltpu.CompilerParams(vmem_limit_bytes=48 * 1024 * 1024)


def at_device(half, y, z, core):
    return (half * SYH + y) * SZ + z * 2 + core


PENCIL = ("sy", "sz")
HALVES, PAIRS, CORES = range(2), range(SZ // 4), range(2)
SAME_HALF = [[half * BLOCKS + i for i in range(BLOCKS)] for half in HALVES]
FOURS = [
    [at_device(half, y, 2 * pair + odd, core) for odd in HALVES for core in CORES]
    for half in HALVES for y in range(SYH) for pair in PAIRS
]
FAR_FOURS = [
    [at_device(half, y, 2 * pair + odd, core) for pair in PAIRS]
    for half in HALVES for y in range(SYH) for odd in HALVES for core in CORES
]
SIXTEENS = [
    [at_device(half, y, 2 * pair + odd, core) for y in range(SYH) for odd in HALVES for core in CORES]
    for half in HALVES for pair in PAIRS
]


def along_z(step):
    pairs = []
    for half in HALVES:
        for y in range(SYH):
            for z in range(SZ):
                to = (half * SZ + z + step) % (2 * SZ)
                pairs.append((half * SYH * SZ + y * SZ + z, (to // SZ) * SYH * SZ + y * SZ + to % SZ))
    return pairs


def lanes_of(shape):
    return lax.broadcasted_iota(jnp.int32, shape, len(shape) - 1)


def turned(x, shift):
    return pltpu.roll(x, shift % x.shape[-1], x.ndim - 1)


def call(kernel, out_shape, scratch, *args):
    return pl.pallas_call(
        kernel, out_shape=out_shape, scratch_shapes=scratch, compiler_params=PARAMS
    )(*args)


def pack_kernel(near_ref, far_ref, first_ref, second_ref, out_ref, held, filters):
    filters[...] = jnp.zeros_like(filters)
    filters[:, 0:COLUMNS] = first_ref[...]
    filters[:, HALF : HALF + COLUMNS] = second_ref[...]
    share = lax.axis_index("sy") % SYH
    for tile in range(TILES):
        first = pl.multiple_of((share * TILES + tile) * 128, 128)
        columns = filters[:, pl.ds(first, 128)]
        for k in range(BLOCKS):
            out_ref[k, 64 + 16 * tile : 80 + 16 * tile, :] = columns
    lower = lax.axis_index("sy") < SYH
    near, far = near_ref[...].astype(F32), far_ref[...].astype(F32)
    held[0:256, :] = jnp.where(lower, near, far)
    held[256:512, :] = jnp.where(lower, far, near)
    rows = [held[pl.ds(yz, 64, stride=8), :] for yz in range(8)]
    slot = lanes_of((64, 128)) // 16
    for k in range(BLOCKS):
        total = turned(rows[0], RIM - XB * k)
        for yz in range(1, 8):
            total = jnp.where(slot == yz, turned(rows[yz], 16 * yz + RIM - XB * k), total)
        out_ref[k, 0:64, :] = total.astype(BF)


def unpack_kernel(in_ref, out_ref, held):
    for sy in range(SY):
        top = (sy // SYH) * 32
        block = jnp.concatenate(
            [
                in_ref[(sy % SYH) * FILT + f, top + 16 * vc : top + 16 * vc + 16, :]
                for vc in range(2) for f in range(FILT)
            ],
            axis=0,
        )
        flipped = jnp.transpose(block.astype(F32))
        for yy in range(2):
            for z in range(ZB):
                first = (yy * ZB + z) * XW
                held[pl.ds(z * PLANE + 2 * sy + yy, XW, stride=Y), :] = flipped[first : first + XW, :]
    out_ref[...] = held[...].astype(BF)


def y_taps(x):
    cells = x.shape[0] // Y
    split = x.reshape(cells, Y, 128)
    before = pltpu.roll(split, 1, 1).reshape(x.shape)
    after = pltpu.roll(split, Y - 1, 1).reshape(x.shape)
    return before, after


def store_taps(ref, z, x):
    before, after = y_taps(x)
    low = lanes_of(x.shape) < C
    ref[z, :, 0:128] = jnp.where(low, before, x).astype(BF)
    ref[z, :, 128:256] = after.astype(BF)


def softplus(x):
    return jnp.maximum(x, 0.0) + jnp.log1p(jnp.exp(-jnp.abs(x)))


def sigmoid(x):
    e = jnp.exp(-jnp.abs(x))
    return jnp.where(x >= 0, 1.0, e) / (1.0 + e)


def tap_column(a, b, c):
    return (9 * a + 3 * b + c) * C


def filter_block(windows_ref, layer, f, a, b, c):
    column = layer * HALF + tap_column(a, b, c)
    tile = column // 128
    top = 64 + 16 * (tile % TILES)
    return windows_ref[(tile // TILES) * FILT + f, top : top + 16, column % 128 : column % 128 + C]


def fill_forward(ref, windows_ref, layer):
    ref[...] = jnp.zeros_like(ref)
    for b in range(3):
        for a in range(3):
            for at, c in ((0, 0), (1, 1), (2, 2), (3, 2)):
                for f in range(FILT):
                    row = at * C + f * 16
                    ref[row : row + 16, b * 256 + a * C : b * 256 + a * C + C] = filter_block(
                        windows_ref, layer, f, a, b, c
                    )


def fill_backward(ref, windows_ref, layer):
    ref[...] = jnp.zeros_like(ref)
    for b in range(3):
        for a in range(3):
            for at, c in ((0, 0), (1, 1), (2, 2), (3, 2)):
                for f in range(FILT):
                    row = b * 256 + a * C + f * 16
                    ref[row : row + 16, at * C : at * C + C] = filter_block(
                        windows_ref, layer, f, 2 - a, 2 - b, 2 - c
                    )


def convolved(taps_ref, weights, z, wide, transposed):
    rows = wide * Y
    planes = jnp.concatenate([taps_ref[z + b, 0:rows, :] for b in range(3)], axis=1)
    dims = (((1,), (1 if transposed else 0,)), ((), ()))
    sums = lax.dot_general(planes, weights, dims, preferred_element_type=F32)
    left, right = sums[:, 0:128], sums[:, 128:256]
    swapped = turned(left, C)
    kept = rows - 2 * Y
    low = lanes_of((kept, 128)) < C
    return (
        jnp.where(
            low,
            left[0:kept] + swapped[Y : Y + kept],
            left[Y : Y + kept] + swapped[0:kept],
        )
        + right[2 * Y : 2 * Y + kept]
    )


def main_kernel(
    below_ref, own_ref, above_ref, windows_ref, out_ref,
    field, act, delta_2, delta_1, pre_1, cells_0, cells_1, cells_2, cells_3, weights, weights_t,
):
    half = lax.axis_index("sy") // SYH
    slabs = (below_ref, own_ref, above_ref)

    def slab_rows(z, first, count):
        start = (z % ZB) * PLANE + first
        return slabs[z // ZB][start : start + count, :].astype(F32)

    for layer in range(2):
        fill_forward(weights.at[layer], windows_ref, layer)
        fill_backward(weights_t.at[layer], windows_ref, layer)
    for z in range(12):
        x = slab_rows(z, 0, PLANE)
        before, after = y_taps(x)
        low = lanes_of(x.shape) < C
        field[z, :, 0:128] = jnp.where(low, before, turned(x, C)).astype(BF)
        field[z, :, 128:256] = after.astype(BF)
    for z in range(10):
        pre = convolved(field, weights[0], z, XW, True)
        pre_1[z] = pre
        store_taps(act, z, softplus(pre).astype(BF).astype(F32))
    for z in range(8):
        pre = convolved(act, weights[1], z, XW - 2, True)
        cotangent = slab_rows(z + 2, 2 * Y, (XW - 4) * Y)
        low = lanes_of(cotangent.shape) < C
        cotangent = jnp.where(low, turned(cotangent, C), cotangent)
        delta = (cotangent * sigmoid(pre)).astype(BF).astype(F32)
        store_taps(delta_2, z, delta)
        if 2 <= z < 6:
            cells_0[z - 2] = softplus(pre[2 * Y : (2 + XB) * Y])
            cells_2[z - 2] = delta[2 * Y : (2 + XB) * Y]
    for z in range(6):
        back = convolved(delta_2, weights_t[1], z, XW - 4, False)
        delta = (back * sigmoid(pre_1[z + 2, 2 * Y : (XW - 4) * Y, :])).astype(BF).astype(F32)
        store_taps(delta_1, z, delta)
        if 1 <= z < 5:
            cells_3[z - 1] = delta[Y : (1 + XB) * Y]
    for z in range(4):
        cells_1[z] = convolved(delta_1, weights_t[0], z, XW - 6, False)

    count = ZB * XB * Y
    row = lax.broadcasted_iota(jnp.int32, (count, count // 2), 0)
    col = lax.broadcasted_iota(jnp.int32, (count, count // 2), 1)
    y = row % Y - half * (Y // 2)
    order = (y // 2) * 64 + (row // (XB * Y)) * 16 + (y % 2) * XB + (row // Y) % XB
    inside = (y >= 0) & (y < Y // 2)
    reorder = jnp.where(inside & (order == col), 1.0, 0.0).astype(BF)
    for at, cells in enumerate((cells_0, cells_1)):
        flat = jnp.transpose(cells[...].reshape(count, 128))[0:C, :].astype(BF)
        flat = jnp.dot(flat, reorder, preferred_element_type=F32).astype(BF)
        for to in range(SYH):
            first = QUARTER + at * 64
            out_ref[to, :, first : first + 64] = flat[:, to * 64 : to * 64 + 64]
    for base, cells, source, at in ((0, cells_3, field, 3), (HALF, cells_2, act, 2)):
        flat = jnp.transpose(cells[...].reshape(count, 128))[0:C, :].astype(BF)
        for b in range(3):
            for c in range(3):
                near = slice((at + c) * Y, (at + c + XB) * Y)
                near = jnp.concatenate([source[at + b + z, near, :] for z in range(ZB)], axis=0)
                sums = jnp.dot(flat, near, preferred_element_type=F32).astype(BF)
                for a in range(3):
                    first = base + tap_column(a, b, c)
                    to, first = first // QUARTER, first % QUARTER
                    out_ref[to, :, first : first + C] = sums[:, a * C : a * C + C]
        out_ref[(base + COLUMNS) // QUARTER, :, (base + COLUMNS) % QUARTER : QUARTER] = jnp.zeros(
            (C, HALF - COLUMNS), BF
        )


def split_kernel(in_ref, out_ref):
    for to in range(4):
        wide = min(PIECE, QUARTER - to * PIECE)
        lanes = slice(to * PIECE, to * PIECE + wide)
        total = in_ref[0, :, lanes].astype(F32)
        for k in range(1, BLOCKS):
            total = total + in_ref[k, :, lanes].astype(F32)
        out_ref[to, :, 0:wide] = total.astype(BF)
        if wide < PIECE:
            out_ref[to, :, wide:PIECE] = jnp.zeros((16, PIECE - wide), BF)


def outputs_kernel(in_ref, result_ref, grad_input_ref, held):
    blocks = [in_ref[k, :, QUARTER : QUARTER + 128].astype(F32) for k in range(BLOCKS)]
    slot = lanes_of((16, 128)) // XB
    for at, ref in enumerate((result_ref, grad_input_ref)):
        for z in range(ZB):
            for yy in range(2):
                first = at * 64 + z * 16 + yy * XB
                total = turned(blocks[0], -first)
                for k in range(1, BLOCKS):
                    total = jnp.where(slot == k, turned(blocks[k], k * XB - first), total)
                held[at, pl.ds(yy * ZB + z, 16, stride=8), :] = total
        ref[...] = held[at].astype(BF)


def sum_kernel(in_ref, out_ref):
    total = in_ref[0].astype(F32)
    for k in range(1, in_ref.shape[0]):
        total = total + in_ref[k].astype(F32)
    total = total.astype(BF)
    for k in range(out_ref.shape[0]):
        out_ref[k] = total


def finish_kernel(factor, in_ref, first_ref, second_ref):
    for base, ref in ((0, first_ref), (8, second_ref)):
        for k in range(8):
            first = (k // 4) * QUARTER + (k % 4) * PIECE
            wide = min(PIECE, QUARTER - (k % 4) * PIECE, COLUMNS - first)
            ref[:, first : first + wide] = in_ref[base + k, :, 0:wide].astype(F32) * factor


def body(volume, first_filters, second_filters, cotangent):
    shape = jax.ShapeDtypeStruct
    factor = float(SY * volume.shape[1] * SZ * volume.shape[2] * volume.shape[3]) ** -0.5
    with jax.named_scope("halves_exchange"):
        near = jnp.concatenate([volume.reshape(128, 128), cotangent.reshape(128, 128)], axis=0)
        far = lax.ppermute(near, "sy", [(i, (i + SYH) % SY) for i in range(SY)])
    with jax.named_scope("pack_windows"):
        packed = call(
            pack_kernel,
            shape((BLOCKS, 64 + 16 * TILES, 128), BF),
            [pltpu.VMEM((512, 128), F32), pltpu.VMEM((16, 2 * HALF), BF)],
            near, far, first_filters, second_filters,
        )
    with jax.named_scope("windows_exchange"):
        windows = lax.all_to_all(packed, ("sy", "filt"), 0, 0, tiled=True, axis_index_groups=SAME_HALF)
    with jax.named_scope("unpack_windows"):
        own = call(unpack_kernel, shape((ZB * PLANE, 128), BF), [pltpu.VMEM((ZB * PLANE, 128), F32)], windows)
    with jax.named_scope("z_rim_exchange"):
        below = lax.ppermute(own, PENCIL, along_z(1))
        above = lax.ppermute(own, PENCIL, along_z(-1))
    with jax.named_scope("layers"):
        partial = call(
            main_kernel,
            shape((SYH, C, QUARTER + 128), BF),
            [
                pltpu.VMEM((12, XW * Y, 256), BF),
                pltpu.VMEM((10, (XW - 2) * Y, 256), BF),
                pltpu.VMEM((8, (XW - 4) * Y, 256), BF),
                pltpu.VMEM((6, (XW - 6) * Y, 256), BF),
                pltpu.VMEM((10, (XW - 2) * Y, 128), F32),
                pltpu.VMEM((ZB, XB * Y, 128), F32),
                pltpu.VMEM((ZB, XB * Y, 128), F32),
                pltpu.VMEM((ZB, XB * Y, 128), F32),
                pltpu.VMEM((ZB, XB * Y, 128), F32),
                pltpu.VMEM((2, 256, 768), BF),
                pltpu.VMEM((2, 768, 256), BF),
            ],
            below, own, above, windows,
        )
    with jax.named_scope("blocks_exchange"):
        shares = partial.reshape(BLOCKS, 16, QUARTER + 128)
        shares = lax.all_to_all(shares, ("sy", "filt"), 0, 0, tiled=True, axis_index_groups=SAME_HALF)
    with jax.named_scope("split_shares"):
        pieces = call(split_kernel, shape((4, 16, PIECE), BF), [], shares)
    with jax.named_scope("place_outputs"):
        result, grad_input = call(
            outputs_kernel,
            (shape((128, 128), BF), shape((128, 128), BF)),
            [pltpu.VMEM((2, 128, 128), F32)],
            shares,
        )
    with jax.named_scope("near_sum_exchange"):
        pieces = lax.all_to_all(pieces, PENCIL, 0, 0, tiled=True, axis_index_groups=FOURS)
        pieces = call(sum_kernel, shape((4, 16, PIECE), BF), [], pieces)
    with jax.named_scope("far_sum_exchange"):
        pieces = lax.all_to_all(pieces, PENCIL, 0, 0, tiled=True, axis_index_groups=FAR_FOURS)
        pieces = call(sum_kernel, shape((16, 16, PIECE), BF), [], pieces)
    with jax.named_scope("spread_exchange"):
        pieces = lax.all_to_all(pieces, PENCIL, 0, 0, tiled=True, axis_index_groups=SIXTEENS)
    with jax.named_scope("finish"):
        first_grad, second_grad = call(
            lambda *refs: finish_kernel(factor, *refs),
            (shape((16, COLUMNS), F32), shape((16, COLUMNS), F32)),
            [],
            pieces,
        )
    return (result.reshape(volume.shape), grad_input.reshape(volume.shape), first_grad, second_grad)


def solution(mesh):
    return jax.shard_map(
        body,
        mesh=mesh,
        in_specs=(
            P("filt", "sy", "sz", None),
            P("filt", None),
            P("filt", None),
            P("filt", "sy", "sz", None),
        ),
        out_specs=(
            P("filt", "sy", "sz", None),
            P("filt", "sy", "sz", None),
            P("filt", None),
            P("filt", None),
        ),
        check_vma=False,
    )
```

```python
import jax
import jax.numpy as jnp
from jax import lax
from jax.experimental import pallas as pl
from jax.experimental.pallas import tpu as pltpu
from jax.sharding import PartitionSpec as P

BF = jnp.bfloat16
F32 = jnp.float32
C = 64
Y = 16
SY = 8
SZ = 16
FILT = 4
SYH = SY // 2
ZB = 4
XB = 8
RIM = 4
XW = XB + 2 * RIM
PLANE = XW * Y
BLOCKS = SYH * FILT
HALF = 28 * C
GRADS = 2 * HALF
QUARTER = GRADS // SYH
PIECE = 256
COLUMNS = 27 * C
PARAMS = pltpu.CompilerParams(vmem_limit_bytes=48 * 1024 * 1024)


def at_device(half, y, z, core):
    return (half * SYH + y) * SZ + z * 2 + core


PENCIL = ("sy", "sz")
HALVES, PAIRS, CORES = range(2), range(SZ // 4), range(2)
SAME_HALF = [[half * BLOCKS + i for i in range(BLOCKS)] for half in HALVES]
FOURS = [
    [at_device(half, y, 2 * pair + odd, core) for odd in HALVES for core in CORES]
    for half in HALVES for y in range(SYH) for pair in PAIRS
]
FAR_FOURS = [
    [at_device(half, y, 2 * pair + odd, core) for pair in PAIRS]
    for half in HALVES for y in range(SYH) for odd in HALVES for core in CORES
]
SIXTEENS = [
    [at_device(half, y, 2 * pair + odd, core) for y in range(SYH) for odd in HALVES for core in CORES]
    for half in HALVES for pair in PAIRS
]


def along_z(step):
    pairs = []
    for half in HALVES:
        for y in range(SYH):
            for z in range(SZ):
                to = (half * SZ + z + step) % (2 * SZ)
                pairs.append((half * SYH * SZ + y * SZ + z, (to // SZ) * SYH * SZ + y * SZ + to % SZ))
    return pairs


def lanes_of(shape):
    return lax.broadcasted_iota(jnp.int32, shape, len(shape) - 1)


def turned(x, shift):
    return pltpu.roll(x, shift % x.shape[-1], x.ndim - 1)


def call(kernel, out_shape, scratch, *args):
    return pl.pallas_call(
        kernel, out_shape=out_shape, scratch_shapes=scratch, compiler_params=PARAMS
    )(*args)


def pack_kernel(near_ref, far_ref, out_ref, held):
    lower = lax.axis_index("sy") < SYH
    near, far = near_ref[...].astype(F32), far_ref[...].astype(F32)
    held[0:256, :] = jnp.where(lower, near, far)
    held[256:512, :] = jnp.where(lower, far, near)
    rows = [held[pl.ds(yz, 64, stride=8), :] for yz in range(8)]
    slot = lanes_of((64, 128)) // 16
    for k in range(BLOCKS):
        total = turned(rows[0], RIM - XB * k)
        for yz in range(1, 8):
            total = jnp.where(slot == yz, turned(rows[yz], 16 * yz + RIM - XB * k), total)
        out_ref[k] = total.astype(BF)


def unpack_kernel(in_ref, out_ref, held):
    for sy in range(SY):
        top = (sy // SYH) * 32
        block = jnp.concatenate(
            [
                in_ref[(sy % SYH) * FILT + f, top + 16 * vc : top + 16 * vc + 16, :]
                for vc in range(2) for f in range(FILT)
            ],
            axis=0,
        )
        flipped = jnp.transpose(block.astype(F32))
        for yy in range(2):
            for z in range(ZB):
                first = (yy * ZB + z) * XW
                held[pl.ds(z * PLANE + 2 * sy + yy, XW, stride=Y), :] = flipped[first : first + XW, :]
    out_ref[...] = held[...].astype(BF)


def y_taps(x):
    cells = x.shape[0] // Y
    split = x.reshape(cells, Y, 128)
    before = pltpu.roll(split, 1, 1).reshape(x.shape)
    after = pltpu.roll(split, Y - 1, 1).reshape(x.shape)
    return before, after


def store_taps(ref, z, x):
    before, after = y_taps(x)
    low = lanes_of(x.shape) < C
    ref[z, :, 0:128] = jnp.where(low, before, x).astype(BF)
    ref[z, :, 128:256] = after.astype(BF)


def store_field(ref, at, slab_ref, z):
    x = slab_ref[z * PLANE : (z + 1) * PLANE, :].astype(F32)
    before, after = y_taps(x)
    low = lanes_of(x.shape) < C
    ref[at, :, 0:128] = jnp.where(low, before, turned(x, C)).astype(BF)
    ref[at, :, 128:256] = after.astype(BF)


def softplus(x):
    return jnp.maximum(x, 0.0) + jnp.log1p(jnp.exp(-jnp.abs(x)))


def sigmoid(x):
    e = jnp.exp(-jnp.abs(x))
    return jnp.where(x >= 0, 1.0, e) / (1.0 + e)


def tap_column(a, b, c):
    return (9 * a + 3 * b + c) * C


def filter_block(filters_ref, layer, f, a, b, c):
    first = tap_column(a, b, c)
    return filters_ref[f, layer, :, first : first + C]


def fill_forward(ref, filters_ref, layer):
    ref[...] = jnp.zeros_like(ref)
    for b in range(3):
        for a in range(3):
            for at, c in ((0, 0), (1, 1), (2, 2), (3, 2)):
                for f in range(FILT):
                    row = at * C + f * 16
                    ref[row : row + 16, b * 256 + a * C : b * 256 + a * C + C] = filter_block(
                        filters_ref, layer, f, a, b, c
                    )


def fill_backward(ref, filters_ref, layer):
    ref[...] = jnp.zeros_like(ref)
    for b in range(3):
        for a in range(3):
            for at, c in ((0, 0), (1, 1), (2, 2), (3, 2)):
                for f in range(FILT):
                    row = b * 256 + a * C + f * 16
                    ref[row : row + 16, at * C : at * C + C] = filter_block(
                        filters_ref, layer, f, 2 - a, 2 - b, 2 - c
                    )


def prepare_kernel(own_ref, filters_ref, weights, weights_t, field):
    for layer in range(2):
        fill_forward(weights.at[layer], filters_ref, layer)
        fill_backward(weights_t.at[layer], filters_ref, layer)
    for z in range(ZB):
        store_field(field, z, own_ref, z)


def convolved(planes, weights, transposed):
    rows = planes[0].shape[0]
    planes = jnp.concatenate(planes, axis=1)
    dims = (((1,), (1 if transposed else 0,)), ((), ()))
    sums = lax.dot_general(planes, weights, dims, preferred_element_type=F32)
    left, right = sums[:, 0:128], sums[:, 128:256]
    swapped = turned(left, C)
    kept = rows - 2 * Y
    low = lanes_of((kept, 128)) < C
    return (
        jnp.where(
            low,
            left[0:kept] + swapped[Y : Y + kept],
            left[Y : Y + kept] + swapped[0:kept],
        )
        + right[2 * Y : 2 * Y + kept]
    )


def main_kernel(
    below_ref, own_ref, above_ref, weights, weights_t, field_own, out_ref,
    field, act, delta_2, delta_1, pre_1, cells_0, cells_1, cells_2, cells_3,
):
    half = lax.axis_index("sy") // SYH
    slabs = (below_ref, own_ref, above_ref)

    def slab_rows(z, first, count):
        start = (z % ZB) * PLANE + first
        return slabs[z // ZB][start : start + count, :].astype(F32)

    def field_rows(z, rows):
        if ZB <= z < 2 * ZB:
            return field_own[z - ZB, rows, :]
        return field[z if z < ZB else z - ZB, rows, :]

    def planes(ref, z):
        return [ref[z + b] for b in range(3)]

    for z in range(ZB):
        store_field(field, z, below_ref, z)
        store_field(field, ZB + z, above_ref, z)
    for z in range(10):
        pre = convolved([field_rows(z + b, slice(0, PLANE)) for b in range(3)], weights[0], True)
        pre_1[z] = pre
        store_taps(act, z, softplus(pre).astype(BF).astype(F32))
    for z in range(8):
        pre = convolved(planes(act, z), weights[1], True)
        cotangent = slab_rows(z + 2, 2 * Y, (XW - 4) * Y)
        low = lanes_of(cotangent.shape) < C
        cotangent = jnp.where(low, turned(cotangent, C), cotangent)
        delta = (cotangent * sigmoid(pre)).astype(BF).astype(F32)
        store_taps(delta_2, z, delta)
        if 2 <= z < 6:
            cells_0[z - 2] = softplus(pre[2 * Y : (2 + XB) * Y])
            cells_2[z - 2] = delta[2 * Y : (2 + XB) * Y]
    for z in range(6):
        back = convolved(planes(delta_2, z), weights_t[1], False)
        delta = (back * sigmoid(pre_1[z + 2, 2 * Y : (XW - 4) * Y, :])).astype(BF).astype(F32)
        store_taps(delta_1, z, delta)
        if 1 <= z < 5:
            cells_3[z - 1] = delta[Y : (1 + XB) * Y]
    for z in range(4):
        cells_1[z] = convolved(planes(delta_1, z), weights_t[0], False)

    count = ZB * XB * Y
    row = lax.broadcasted_iota(jnp.int32, (count, count // 2), 0)
    col = lax.broadcasted_iota(jnp.int32, (count, count // 2), 1)
    y = row % Y - half * (Y // 2)
    order = (y // 2) * 64 + (row // (XB * Y)) * 16 + (y % 2) * XB + (row // Y) % XB
    inside = (y >= 0) & (y < Y // 2)
    reorder = jnp.where(inside & (order == col), 1.0, 0.0).astype(BF)
    for at, cells in enumerate((cells_0, cells_1)):
        flat = jnp.transpose(cells[...].reshape(count, 128))[0:C, :].astype(BF)
        flat = jnp.dot(flat, reorder, preferred_element_type=F32).astype(BF)
        for to in range(SYH):
            first = QUARTER + at * 64
            out_ref[to, :, first : first + 64] = flat[:, to * 64 : to * 64 + 64]
    def act_rows(z, rows):
        return act[z, rows, :]

    for base, cells, source, at in ((0, cells_3, field_rows, 3), (HALF, cells_2, act_rows, 2)):
        flat = jnp.transpose(cells[...].reshape(count, 128))[0:C, :].astype(BF)
        for b in range(3):
            for c in range(3):
                near = slice((at + c) * Y, (at + c + XB) * Y)
                near = jnp.concatenate([source(at + b + z, near) for z in range(ZB)], axis=0)
                sums = jnp.dot(flat, near, preferred_element_type=F32).astype(BF)
                for a in range(3):
                    first = base + tap_column(a, b, c)
                    to, first = first // QUARTER, first % QUARTER
                    out_ref[to, :, first : first + C] = sums[:, a * C : a * C + C]
        out_ref[(base + COLUMNS) // QUARTER, :, (base + COLUMNS) % QUARTER : QUARTER] = jnp.zeros(
            (C, HALF - COLUMNS), BF
        )


def split_kernel(in_ref, out_ref, result_ref, grad_input_ref, held):
    for to in range(4):
        wide = min(PIECE, QUARTER - to * PIECE)
        lanes = slice(to * PIECE, to * PIECE + wide)
        total = in_ref[0, :, lanes].astype(F32)
        for k in range(1, BLOCKS):
            total = total + in_ref[k, :, lanes].astype(F32)
        out_ref[to, :, 0:wide] = total.astype(BF)
        if wide < PIECE:
            out_ref[to, :, wide:PIECE] = jnp.zeros((16, PIECE - wide), BF)
    blocks = [in_ref[k, :, QUARTER : QUARTER + 128].astype(F32) for k in range(BLOCKS)]
    slot = lanes_of((16, 128)) // XB
    for bit in (1, 2, 4, 8):
        clear = slot & bit == 0
        blocks = [
            jnp.where(clear, turned(blocks[k - bit], -bit * XB), blocks[k])
            if k & bit
            else jnp.where(clear, blocks[k], turned(blocks[k + bit], bit * XB))
            for k in range(BLOCKS)
        ]
    for at, ref in enumerate((result_ref, grad_input_ref)):
        for z in range(ZB):
            for yy in range(2):
                held[at, pl.ds(yy * ZB + z, 16, stride=8), :] = blocks[at * 8 + z * 2 + yy]
        ref[...] = held[at].astype(BF)


def sum_kernel(in_ref, out_ref):
    total = in_ref[0].astype(F32)
    for k in range(1, in_ref.shape[0]):
        total = total + in_ref[k].astype(F32)
    total = total.astype(BF)
    for k in range(out_ref.shape[0]):
        out_ref[k] = total


def finish_kernel(factor, in_ref, first_ref, second_ref):
    for base, ref in ((0, first_ref), (8, second_ref)):
        for k in range(8):
            first = (k // 4) * QUARTER + (k % 4) * PIECE
            wide = min(PIECE, QUARTER - (k % 4) * PIECE, COLUMNS - first)
            ref[:, first : first + wide] = in_ref[base + k, :, 0:wide].astype(F32) * factor


def body(volume, first_filters, second_filters, cotangent):
    shape = jax.ShapeDtypeStruct
    factor = float(SY * volume.shape[1] * SZ * volume.shape[2] * volume.shape[3]) ** -0.5
    with jax.named_scope("halves_exchange"):
        near = jnp.concatenate([volume.reshape(128, 128), cotangent.reshape(128, 128)], axis=0)
        far = lax.ppermute(near, "sy", [(i, (i + SYH) % SY) for i in range(SY)])
    with jax.named_scope("pack_windows"):
        packed = pl.pallas_call(
            pack_kernel,
            out_shape=shape((BLOCKS, 64, 128), BF),
            scratch_shapes=[pltpu.VMEM((512, 128), F32)],
            compiler_params=PARAMS,
            cost_estimate=pl.CostEstimate(flops=40_000_000_000, bytes_accessed=1_000_000, transcendentals=0),
        )(near, far)
    with jax.named_scope("filters_exchange"):
        filters = jnp.broadcast_to(jnp.stack([first_filters, second_filters]), (FILT, 2, 16, COLUMNS))
        filters = lax.all_to_all(filters, "filt", 0, 0, tiled=True)
        packed, filters = lax.optimization_barrier((packed, filters))
    with jax.named_scope("windows_exchange"):
        windows = lax.all_to_all(packed, ("sy", "filt"), 0, 0, tiled=True, axis_index_groups=SAME_HALF)
    with jax.named_scope("unpack_windows"):
        own = call(unpack_kernel, shape((ZB * PLANE, 128), BF), [pltpu.VMEM((ZB * PLANE, 128), F32)], windows)
    with jax.named_scope("z_rim_exchange"):
        below = lax.ppermute(own, PENCIL, along_z(1))
        above = lax.ppermute(own, PENCIL, along_z(-1))
    with jax.named_scope("prepare"):
        weights, weights_t, field_own = call(
            prepare_kernel,
            (shape((2, 256, 768), BF), shape((2, 768, 256), BF), shape((ZB, PLANE, 256), BF)),
            [],
            own, filters,
        )
    with jax.named_scope("layers"):
        partial = call(
            main_kernel,
            shape((SYH, C, QUARTER + 128), BF),
            [
                pltpu.VMEM((8, XW * Y, 256), BF),
                pltpu.VMEM((10, (XW - 2) * Y, 256), BF),
                pltpu.VMEM((8, (XW - 4) * Y, 256), BF),
                pltpu.VMEM((6, (XW - 6) * Y, 256), BF),
                pltpu.VMEM((10, (XW - 2) * Y, 128), F32),
                pltpu.VMEM((ZB, XB * Y, 128), F32),
                pltpu.VMEM((ZB, XB * Y, 128), F32),
                pltpu.VMEM((ZB, XB * Y, 128), F32),
                pltpu.VMEM((ZB, XB * Y, 128), F32),
            ],
            below, own, above, weights, weights_t, field_own,
        )
    with jax.named_scope("blocks_exchange"):
        shares = partial.reshape(BLOCKS, 16, QUARTER + 128)
        shares = lax.all_to_all(shares, ("sy", "filt"), 0, 0, tiled=True, axis_index_groups=SAME_HALF)
    with jax.named_scope("split_shares"):
        pieces, result, grad_input = call(
            split_kernel,
            (shape((4, 16, PIECE), BF), shape((128, 128), BF), shape((128, 128), BF)),
            [pltpu.VMEM((2, 128, 128), F32)],
            shares,
        )
    with jax.named_scope("near_sum_exchange"):
        pieces = lax.all_to_all(pieces, PENCIL, 0, 0, tiled=True, axis_index_groups=FOURS)
        pieces = call(sum_kernel, shape((4, 16, PIECE), BF), [], pieces)
    with jax.named_scope("far_sum_exchange"):
        pieces = lax.all_to_all(pieces, PENCIL, 0, 0, tiled=True, axis_index_groups=FAR_FOURS)
        pieces = call(sum_kernel, shape((16, 16, PIECE), BF), [], pieces)
    with jax.named_scope("spread_exchange"):
        pieces = lax.all_to_all(pieces, PENCIL, 0, 0, tiled=True, axis_index_groups=SIXTEENS)
    with jax.named_scope("finish"):
        first_grad, second_grad = call(
            lambda *refs: finish_kernel(factor, *refs),
            (shape((16, COLUMNS), F32), shape((16, COLUMNS), F32)),
            [],
            pieces,
        )
    return (result.reshape(volume.shape), grad_input.reshape(volume.shape), first_grad, second_grad)


def solution(mesh):
    return jax.shard_map(
        body,
        mesh=mesh,
        in_specs=(
            P("filt", "sy", "sz", None),
            P("filt", None),
            P("filt", None),
            P("filt", "sy", "sz", None),
        ),
        out_specs=(
            P("filt", "sy", "sz", None),
            P("filt", "sy", "sz", None),
            P("filt", None),
            P("filt", None),
        ),
        check_vma=False,
    )
```

```python
import jax
import jax.numpy as jnp
from jax import lax
from jax.experimental import pallas as pl
from jax.experimental.pallas import tpu as pltpu
from jax.sharding import PartitionSpec as P

BF = jnp.bfloat16
F32 = jnp.float32
C = 64
Y = 16
SY = 8
SZ = 16
FILT = 4
SYH = SY // 2
ZB = 4
XB = 8
RIM = 4
XW = XB + 2 * RIM
PLANE = XW * Y
BLOCKS = SYH * FILT
HALF = 28 * C
GRADS = 2 * HALF
QUARTER = GRADS // SYH
PIECE = 256
COLUMNS = 27 * C
PARAMS = pltpu.CompilerParams(vmem_limit_bytes=48 * 1024 * 1024)


def at_device(half, y, z, core):
    return (half * SYH + y) * SZ + z * 2 + core


PENCIL = ("sy", "sz")
HALVES, PAIRS, CORES = range(2), range(SZ // 4), range(2)
SAME_HALF = [[half * BLOCKS + i for i in range(BLOCKS)] for half in HALVES]
FOURS = [
    [at_device(half, y, 2 * pair + odd, core) for odd in HALVES for core in CORES]
    for half in HALVES for y in range(SYH) for pair in PAIRS
]
FAR_FOURS = [
    [at_device(half, y, 2 * pair + odd, core) for pair in PAIRS]
    for half in HALVES for y in range(SYH) for odd in HALVES for core in CORES
]
SIXTEENS = [
    [at_device(half, y, 2 * pair + odd, core) for y in range(SYH) for odd in HALVES for core in CORES]
    for half in HALVES for pair in PAIRS
]


def along_z(step):
    pairs = []
    for half in HALVES:
        for y in range(SYH):
            for z in range(SZ):
                to = (half * SZ + z + step) % (2 * SZ)
                pairs.append((half * SYH * SZ + y * SZ + z, (to // SZ) * SYH * SZ + y * SZ + to % SZ))
    return pairs


def lanes_of(shape):
    return lax.broadcasted_iota(jnp.int32, shape, len(shape) - 1)


def turned(x, shift):
    return pltpu.roll(x, shift % x.shape[-1], x.ndim - 1)


def call(kernel, out_shape, scratch, *args):
    return pl.pallas_call(
        kernel, out_shape=out_shape, scratch_shapes=scratch, compiler_params=PARAMS
    )(*args)


def pack_kernel(near_ref, far_ref, out_ref, held):
    lower = lax.axis_index("sy") < SYH
    near, far = near_ref[...].astype(F32), far_ref[...].astype(F32)
    held[0:256, :] = jnp.where(lower, near, far)
    held[256:512, :] = jnp.where(lower, far, near)
    rows = [held[pl.ds(yz, 64, stride=8), :] for yz in range(8)]
    slot = lanes_of((64, 128)) // 16
    for k in range(BLOCKS):
        total = turned(rows[0], RIM - XB * k)
        for yz in range(1, 8):
            total = jnp.where(slot == yz, turned(rows[yz], 16 * yz + RIM - XB * k), total)
        out_ref[k] = total.astype(BF)


def unpack_kernel(in_ref, out_ref, held):
    for sy in range(SY):
        top = (sy // SYH) * 32
        block = jnp.concatenate(
            [
                in_ref[(sy % SYH) * FILT + f, top + 16 * vc : top + 16 * vc + 16, :]
                for vc in range(2) for f in range(FILT)
            ],
            axis=0,
        )
        flipped = jnp.transpose(block.astype(F32))
        for yy in range(2):
            for z in range(ZB):
                first = (yy * ZB + z) * XW
                held[pl.ds(z * PLANE + 2 * sy + yy, XW, stride=Y), :] = flipped[first : first + XW, :]
    out_ref[...] = held[...].astype(BF)


def y_taps(x):
    cells = x.shape[0] // Y
    split = x.reshape(cells, Y, 128)
    before = pltpu.roll(split, 1, 1).reshape(x.shape)
    after = pltpu.roll(split, Y - 1, 1).reshape(x.shape)
    return before, after


def store_taps(ref, z, x):
    before, after = y_taps(x)
    low = lanes_of(x.shape) < C
    ref[z, :, 0:128] = jnp.where(low, before, x).astype(BF)
    ref[z, :, 128:256] = after.astype(BF)


def store_field(ref, at, slab_ref, z):
    x = slab_ref[z * PLANE : (z + 1) * PLANE, :].astype(F32)
    before, after = y_taps(x)
    low = lanes_of(x.shape) < C
    ref[at, :, 0:128] = jnp.where(low, before, turned(x, C)).astype(BF)
    ref[at, :, 128:256] = after.astype(BF)


def softplus(x):
    return jnp.maximum(x, 0.0) + jnp.log1p(jnp.exp(-jnp.abs(x)))


def sigmoid(x):
    e = jnp.exp(-jnp.abs(x))
    return jnp.where(x >= 0, 1.0, e) / (1.0 + e)


def tap_column(a, b, c):
    return (9 * a + 3 * b + c) * C


def filter_block(filters_ref, layer, f, a, b, c):
    first = tap_column(a, b, c)
    return filters_ref[f, layer, :, first : first + C]


def fill_forward(ref, filters_ref, layer):
    ref[...] = jnp.zeros_like(ref)
    for b in range(3):
        for a in range(3):
            for at, c in ((0, 0), (1, 1), (2, 2), (3, 2)):
                for f in range(FILT):
                    row = at * C + f * 16
                    ref[row : row + 16, b * 256 + a * C : b * 256 + a * C + C] = filter_block(
                        filters_ref, layer, f, a, b, c
                    )


def fill_backward(ref, filters_ref, layer):
    ref[...] = jnp.zeros_like(ref)
    for b in range(3):
        for a in range(3):
            for at, c in ((0, 0), (1, 1), (2, 2), (3, 2)):
                for f in range(FILT):
                    row = b * 256 + a * C + f * 16
                    ref[row : row + 16, at * C : at * C + C] = filter_block(
                        filters_ref, layer, f, 2 - a, 2 - b, 2 - c
                    )


def prepare_kernel(own_ref, filters_ref, weights, weights_t, field):
    for layer in range(2):
        fill_forward(weights.at[layer], filters_ref, layer)
        fill_backward(weights_t.at[layer], filters_ref, layer)
    for z in range(ZB):
        store_field(field, z, own_ref, z)


def convolved(planes, weights, transposed):
    rows = planes[0].shape[0]
    planes = jnp.concatenate(planes, axis=1)
    dims = (((1,), (1 if transposed else 0,)), ((), ()))
    sums = lax.dot_general(planes, weights, dims, preferred_element_type=F32)
    left, right = sums[:, 0:128], sums[:, 128:256]
    swapped = turned(left, C)
    kept = rows - 2 * Y
    low = lanes_of((kept, 128)) < C
    return (
        jnp.where(
            low,
            left[0:kept] + swapped[Y : Y + kept],
            left[Y : Y + kept] + swapped[0:kept],
        )
        + right[2 * Y : 2 * Y + kept]
    )


def main_kernel(
    below_ref, own_ref, above_ref, weights, weights_t, field_own, out_ref,
    field, act, delta_2, delta_1, pre_1, cells_0, cells_1, cells_2, cells_3,
):
    half = lax.axis_index("sy") // SYH
    slabs = (below_ref, own_ref, above_ref)

    def slab_rows(z, first, count):
        start = (z % ZB) * PLANE + first
        return slabs[z // ZB][start : start + count, :].astype(F32)

    def field_rows(z, rows):
        if ZB <= z < 2 * ZB:
            return field_own[z - ZB, rows, :]
        return field[z if z < ZB else z - ZB, rows, :]

    def planes(ref, z):
        return [ref[z + b] for b in range(3)]

    for z in range(ZB):
        store_field(field, z, below_ref, z)
        store_field(field, ZB + z, above_ref, z)
    for z in range(10):
        pre = convolved([field_rows(z + b, slice(0, PLANE)) for b in range(3)], weights[0], True)
        pre_1[z] = pre
        store_taps(act, z, softplus(pre).astype(BF).astype(F32))
    for z in range(8):
        pre = convolved(planes(act, z), weights[1], True)
        cotangent = slab_rows(z + 2, 2 * Y, (XW - 4) * Y)
        low = lanes_of(cotangent.shape) < C
        cotangent = jnp.where(low, turned(cotangent, C), cotangent)
        delta = (cotangent * sigmoid(pre)).astype(BF).astype(F32)
        store_taps(delta_2, z, delta)
        if 2 <= z < 6:
            cells_0[z - 2] = softplus(pre[2 * Y : (2 + XB) * Y])
            cells_2[z - 2] = delta[2 * Y : (2 + XB) * Y]
    for z in range(6):
        back = convolved(planes(delta_2, z), weights_t[1], False)
        delta = (back * sigmoid(pre_1[z + 2, 2 * Y : (XW - 4) * Y, :])).astype(BF).astype(F32)
        store_taps(delta_1, z, delta)
        if 1 <= z < 5:
            cells_3[z - 1] = delta[Y : (1 + XB) * Y]
    for z in range(4):
        cells_1[z] = convolved(planes(delta_1, z), weights_t[0], False)

    count = ZB * XB * Y
    row = lax.broadcasted_iota(jnp.int32, (count, count // 2), 0)
    col = lax.broadcasted_iota(jnp.int32, (count, count // 2), 1)
    y = row % Y - half * (Y // 2)
    order = (y // 2) * 64 + (row // (XB * Y)) * 16 + (y % 2) * XB + (row // Y) % XB
    inside = (y >= 0) & (y < Y // 2)
    reorder = jnp.where(inside & (order == col), 1.0, 0.0).astype(BF)
    for at, cells in enumerate((cells_0, cells_1)):
        flat = jnp.transpose(cells[...].reshape(count, 128))[0:C, :].astype(BF)
        flat = jnp.dot(flat, reorder, preferred_element_type=F32).astype(BF)
        for to in range(SYH):
            first = QUARTER + at * 64
            out_ref[to, :, first : first + 64] = flat[:, to * 64 : to * 64 + 64]
    def act_rows(z, rows):
        return act[z, rows, :]

    for base, cells, source, at in ((0, cells_3, field_rows, 3), (HALF, cells_2, act_rows, 2)):
        flat = jnp.transpose(cells[...].reshape(count, 128))[0:C, :].astype(BF)
        for b in range(3):
            for c in range(3):
                near = slice((at + c) * Y, (at + c + XB) * Y)
                near = jnp.concatenate([source(at + b + z, near) for z in range(ZB)], axis=0)
                sums = jnp.dot(flat, near, preferred_element_type=F32).astype(BF)
                for a in range(3):
                    first = base + tap_column(a, b, c)
                    to, first = first // QUARTER, first % QUARTER
                    out_ref[to, :, first : first + C] = sums[:, a * C : a * C + C]
        out_ref[(base + COLUMNS) // QUARTER, :, (base + COLUMNS) % QUARTER : QUARTER] = jnp.zeros(
            (C, HALF - COLUMNS), BF
        )


def split_kernel(in_ref, out_ref):
    for to in range(4):
        wide = min(PIECE, QUARTER - to * PIECE)
        lanes = slice(to * PIECE, to * PIECE + wide)
        total = in_ref[0, :, lanes].astype(F32)
        for k in range(1, BLOCKS):
            total = total + in_ref[k, :, lanes].astype(F32)
        out_ref[to, :, 0:wide] = total.astype(BF)
        if wide < PIECE:
            out_ref[to, :, wide:PIECE] = jnp.zeros((16, PIECE - wide), BF)


def sum_kernel(in_ref, out_ref):
    total = in_ref[0].astype(F32)
    for k in range(1, in_ref.shape[0]):
        total = total + in_ref[k].astype(F32)
    total = total.astype(BF)
    for k in range(out_ref.shape[0]):
        out_ref[k] = total


def finish_kernel(factor, in_ref, shares_ref, result_ref, grad_input_ref, first_ref, second_ref, held):
    for base, ref in ((0, first_ref), (8, second_ref)):
        for k in range(8):
            first = (k // 4) * QUARTER + (k % 4) * PIECE
            wide = min(PIECE, QUARTER - (k % 4) * PIECE, COLUMNS - first)
            ref[:, first : first + wide] = in_ref[base + k, :, 0:wide].astype(F32) * factor
    blocks = [shares_ref[k, :, QUARTER : QUARTER + 128].astype(F32) for k in range(BLOCKS)]
    slot = lanes_of((16, 128)) // XB
    for bit in (1, 2, 4, 8):
        clear = slot & bit == 0
        blocks = [
            jnp.where(clear, turned(blocks[k - bit], -bit * XB), blocks[k])
            if k & bit
            else jnp.where(clear, blocks[k], turned(blocks[k + bit], bit * XB))
            for k in range(BLOCKS)
        ]
    for at, ref in enumerate((result_ref, grad_input_ref)):
        for z in range(ZB):
            for yy in range(2):
                held[at, pl.ds(yy * ZB + z, 16, stride=8), :] = blocks[at * 8 + z * 2 + yy]
        ref[...] = held[at].astype(BF)


def body(volume, first_filters, second_filters, cotangent):
    shape = jax.ShapeDtypeStruct
    factor = float(SY * volume.shape[1] * SZ * volume.shape[2] * volume.shape[3]) ** -0.5
    with jax.named_scope("halves_exchange"):
        near = jnp.concatenate([volume.reshape(128, 128), cotangent.reshape(128, 128)], axis=0)
        far = lax.ppermute(near, "sy", [(i, (i + SYH) % SY) for i in range(SY)])
    with jax.named_scope("pack_windows"):
        packed = pl.pallas_call(
            pack_kernel,
            out_shape=shape((BLOCKS, 64, 128), BF),
            scratch_shapes=[pltpu.VMEM((512, 128), F32)],
            compiler_params=PARAMS,
            cost_estimate=pl.CostEstimate(flops=40_000_000_000, bytes_accessed=1_000_000, transcendentals=0),
        )(near, far)
    with jax.named_scope("filters_exchange"):
        filters = jnp.broadcast_to(jnp.stack([first_filters, second_filters]), (FILT, 2, 16, COLUMNS))
        filters = lax.all_to_all(filters, "filt", 0, 0, tiled=True)
        packed, filters = lax.optimization_barrier((packed, filters))
    with jax.named_scope("windows_exchange"):
        windows = lax.all_to_all(packed, ("sy", "filt"), 0, 0, tiled=True, axis_index_groups=SAME_HALF)
    with jax.named_scope("unpack_windows"):
        own = call(unpack_kernel, shape((ZB * PLANE, 128), BF), [pltpu.VMEM((ZB * PLANE, 128), F32)], windows)
    with jax.named_scope("z_rim_exchange"):
        below = lax.ppermute(own, PENCIL, along_z(1))
        above = lax.ppermute(own, PENCIL, along_z(-1))
    with jax.named_scope("prepare"):
        weights, weights_t, field_own = call(
            prepare_kernel,
            (shape((2, 256, 768), BF), shape((2, 768, 256), BF), shape((ZB, PLANE, 256), BF)),
            [],
            own, filters,
        )
    with jax.named_scope("layers"):
        partial = call(
            main_kernel,
            shape((SYH, C, QUARTER + 128), BF),
            [
                pltpu.VMEM((8, XW * Y, 256), BF),
                pltpu.VMEM((10, (XW - 2) * Y, 256), BF),
                pltpu.VMEM((8, (XW - 4) * Y, 256), BF),
                pltpu.VMEM((6, (XW - 6) * Y, 256), BF),
                pltpu.VMEM((10, (XW - 2) * Y, 128), F32),
                pltpu.VMEM((ZB, XB * Y, 128), F32),
                pltpu.VMEM((ZB, XB * Y, 128), F32),
                pltpu.VMEM((ZB, XB * Y, 128), F32),
                pltpu.VMEM((ZB, XB * Y, 128), F32),
            ],
            below, own, above, weights, weights_t, field_own,
        )
    with jax.named_scope("blocks_exchange"):
        shares = partial.reshape(BLOCKS, 16, QUARTER + 128)
        shares = lax.all_to_all(shares, ("sy", "filt"), 0, 0, tiled=True, axis_index_groups=SAME_HALF)
    with jax.named_scope("split_shares"):
        pieces = call(split_kernel, shape((4, 16, PIECE), BF), [], shares)
    with jax.named_scope("near_sum_exchange"):
        pieces = lax.all_to_all(pieces, PENCIL, 0, 0, tiled=True, axis_index_groups=FOURS)
        pieces = call(sum_kernel, shape((4, 16, PIECE), BF), [], pieces)
    with jax.named_scope("far_sum_exchange"):
        pieces = lax.all_to_all(pieces, PENCIL, 0, 0, tiled=True, axis_index_groups=FAR_FOURS)
        pieces = call(sum_kernel, shape((16, 16, PIECE), BF), [], pieces)
    with jax.named_scope("spread_exchange"):
        pieces = lax.all_to_all(pieces, PENCIL, 0, 0, tiled=True, axis_index_groups=SIXTEENS)
    with jax.named_scope("finish"):
        result, grad_input, first_grad, second_grad = call(
            lambda *refs: finish_kernel(factor, *refs),
            (
                shape((128, 128), BF), shape((128, 128), BF),
                shape((16, COLUMNS), F32), shape((16, COLUMNS), F32),
            ),
            [pltpu.VMEM((2, 128, 128), F32)],
            pieces, shares,
        )
    return (result.reshape(volume.shape), grad_input.reshape(volume.shape), first_grad, second_grad)


def solution(mesh):
    return jax.shard_map(
        body,
        mesh=mesh,
        in_specs=(
            P("filt", "sy", "sz", None),
            P("filt", None),
            P("filt", None),
            P("filt", "sy", "sz", None),
        ),
        out_specs=(
            P("filt", "sy", "sz", None),
            P("filt", "sy", "sz", None),
            P("filt", None),
            P("filt", None),
        ),
        check_vma=False,
    )
```

```python
import jax
import jax.numpy as jnp
from jax import lax
from jax.experimental import pallas as pl
from jax.experimental.pallas import tpu as pltpu
from jax.sharding import PartitionSpec as P

BF = jnp.bfloat16
F32 = jnp.float32
C = 64
Y = 16
SY = 8
SZ = 16
FILT = 4
SYH = SY // 2
ZB = 4
XB = 8
RIM = 4
XW = XB + 2 * RIM
PLANE = XW * Y
BLOCKS = SYH * FILT
HALF = 28 * C
GRADS = 2 * HALF
QUARTER = GRADS // SYH
PIECE = 256
COLUMNS = 27 * C
PARAMS = pltpu.CompilerParams(vmem_limit_bytes=48 * 1024 * 1024)


def at_device(half, y, z, core):
    return (half * SYH + y) * SZ + z * 2 + core


PENCIL = ("sy", "sz")
HALVES, PAIRS, CORES = range(2), range(SZ // 4), range(2)
SAME_HALF = [[half * BLOCKS + i for i in range(BLOCKS)] for half in HALVES]
FOURS = [
    [at_device(half, y, 2 * pair + odd, core) for odd in HALVES for core in CORES]
    for half in HALVES for y in range(SYH) for pair in PAIRS
]
FAR_FOURS = [
    [at_device(half, y, 2 * pair + odd, core) for pair in PAIRS]
    for half in HALVES for y in range(SYH) for odd in HALVES for core in CORES
]
SIXTEENS = [
    [at_device(half, y, 2 * pair + odd, core) for y in range(SYH) for odd in HALVES for core in CORES]
    for half in HALVES for pair in PAIRS
]


def along_z(step):
    pairs = []
    for half in HALVES:
        for y in range(SYH):
            for z in range(SZ):
                to = (half * SZ + z + step) % (2 * SZ)
                pairs.append((half * SYH * SZ + y * SZ + z, (to // SZ) * SYH * SZ + y * SZ + to % SZ))
    return pairs


def lanes_of(shape):
    return lax.broadcasted_iota(jnp.int32, shape, len(shape) - 1)


def turned(x, shift):
    return pltpu.roll(x, shift % x.shape[-1], x.ndim - 1)


def call(kernel, out_shape, scratch, *args):
    return pl.pallas_call(
        kernel, out_shape=out_shape, scratch_shapes=scratch, compiler_params=PARAMS
    )(*args)


def pack_kernel(near_ref, far_ref, out_ref, held):
    lower = lax.axis_index("sy") < SYH
    near, far = near_ref[...].astype(F32), far_ref[...].astype(F32)
    held[0:256, :] = jnp.where(lower, near, far)
    held[256:512, :] = jnp.where(lower, far, near)
    rows = [held[pl.ds(yz, 64, stride=8), :] for yz in range(8)]
    slot = lanes_of((64, 128)) // 16
    for k in range(BLOCKS):
        total = turned(rows[0], RIM - XB * k)
        for yz in range(1, 8):
            total = jnp.where(slot == yz, turned(rows[yz], 16 * yz + RIM - XB * k), total)
        out_ref[k] = total.astype(BF)


def unpack_kernel(in_ref, out_ref, held):
    for sy in range(SY):
        top = (sy // SYH) * 32
        block = jnp.concatenate(
            [
                in_ref[(sy % SYH) * FILT + f, top + 16 * vc : top + 16 * vc + 16, :]
                for vc in range(2) for f in range(FILT)
            ],
            axis=0,
        )
        flipped = jnp.transpose(block.astype(F32))
        for yy in range(2):
            for z in range(ZB):
                first = (yy * ZB + z) * XW
                held[pl.ds(z * PLANE + 2 * sy + yy, XW, stride=Y), :] = flipped[first : first + XW, :]
    out_ref[...] = held[...].astype(BF)


def y_taps(x):
    cells = x.shape[0] // Y
    split = x.reshape(cells, Y, 128)
    before = pltpu.roll(split, 1, 1).reshape(x.shape)
    after = pltpu.roll(split, Y - 1, 1).reshape(x.shape)
    return before, after


def store_taps(ref, z, x):
    before, after = y_taps(x)
    low = lanes_of(x.shape) < C
    ref[z, :, 0:128] = jnp.where(low, before, x).astype(BF)
    ref[z, :, 128:256] = after.astype(BF)


def store_field(ref, at, slab_ref, z):
    x = slab_ref[z * PLANE : (z + 1) * PLANE, :].astype(F32)
    before, after = y_taps(x)
    low = lanes_of(x.shape) < C
    ref[at, :, 0:128] = jnp.where(low, before, turned(x, C)).astype(BF)
    ref[at, :, 128:256] = after.astype(BF)


def softplus(x):
    return jnp.maximum(x, 0.0) + jnp.log1p(jnp.exp(-jnp.abs(x)))


def sigmoid(x):
    e = jnp.exp(-jnp.abs(x))
    return jnp.where(x >= 0, 1.0, e) / (1.0 + e)


def tap_column(a, b, c):
    return (9 * a + 3 * b + c) * C


def filter_block(filters_ref, layer, f, a, b, c):
    first = tap_column(a, b, c)
    return filters_ref[f, layer, :, first : first + C]


def fill_forward(ref, filters_ref, layer):
    ref[...] = jnp.zeros_like(ref)
    for b in range(3):
        for a in range(3):
            for at, c in ((0, 0), (1, 1), (2, 2), (3, 2)):
                for f in range(FILT):
                    row = at * C + f * 16
                    ref[row : row + 16, b * 256 + a * C : b * 256 + a * C + C] = filter_block(
                        filters_ref, layer, f, a, b, c
                    )


def fill_backward(ref, filters_ref, layer):
    ref[...] = jnp.zeros_like(ref)
    for b in range(3):
        for a in range(3):
            for at, c in ((0, 0), (1, 1), (2, 2), (3, 2)):
                for f in range(FILT):
                    row = b * 256 + a * C + f * 16
                    ref[row : row + 16, at * C : at * C + C] = filter_block(
                        filters_ref, layer, f, 2 - a, 2 - b, 2 - c
                    )


def convolved(planes, weights, transposed):
    rows = planes[0].shape[0]
    planes = jnp.concatenate(planes, axis=1)
    dims = (((1,), (1 if transposed else 0,)), ((), ()))
    sums = lax.dot_general(planes, weights, dims, preferred_element_type=F32)
    left, right = sums[:, 0:128], sums[:, 128:256]
    swapped = turned(left, C)
    kept = rows - 2 * Y
    low = lanes_of((kept, 128)) < C
    return (
        jnp.where(
            low,
            left[0:kept] + swapped[Y : Y + kept],
            left[Y : Y + kept] + swapped[0:kept],
        )
        + right[2 * Y : 2 * Y + kept]
    )


def prepare_kernel(own_ref, filters_ref, weights, weights_t, field, pre_own, act_own):
    for layer in range(2):
        fill_forward(weights.at[layer], filters_ref, layer)
        fill_backward(weights_t.at[layer], filters_ref, layer)
    for z in range(ZB):
        store_field(field, z, own_ref, z)
    for at in range(2):
        pre = convolved([field[at + b] for b in range(3)], weights[0], True)
        pre_own[at] = pre
        store_taps(act_own, at, softplus(pre).astype(BF).astype(F32))


def main_kernel(
    below_ref, own_ref, above_ref, weights, weights_t, field_own, pre_own, act_own, out_ref,
    field, act, delta_2, delta_1, pre_1, cells_0, cells_1, cells_2, cells_3,
):
    half = lax.axis_index("sy") // SYH
    slabs = (below_ref, own_ref, above_ref)

    def slab_rows(z, first, count):
        start = (z % ZB) * PLANE + first
        return slabs[z // ZB][start : start + count, :].astype(F32)

    def field_rows(z, rows):
        if ZB <= z < 2 * ZB:
            return field_own[z - ZB, rows, :]
        return field[z if z < ZB else z - ZB, rows, :]

    def planes(ref, z):
        return [ref[z + b] for b in range(3)]

    for z in range(ZB):
        store_field(field, z, below_ref, z)
        store_field(field, ZB + z, above_ref, z)
    def act_rows(z, rows):
        return act_own[z - 4, rows, :] if z in (4, 5) else act[z, rows, :]

    for z in (0, 1, 2, 3, 6, 7, 8, 9):
        pre = convolved([field_rows(z + b, slice(0, PLANE)) for b in range(3)], weights[0], True)
        pre_1[z] = pre
        store_taps(act, z, softplus(pre).astype(BF).astype(F32))
    for z in range(8):
        pre = convolved([act_rows(z + b, slice(None)) for b in range(3)], weights[1], True)
        cotangent = slab_rows(z + 2, 2 * Y, (XW - 4) * Y)
        low = lanes_of(cotangent.shape) < C
        cotangent = jnp.where(low, turned(cotangent, C), cotangent)
        delta = (cotangent * sigmoid(pre)).astype(BF).astype(F32)
        store_taps(delta_2, z, delta)
        if 2 <= z < 6:
            cells_0[z - 2] = softplus(pre[2 * Y : (2 + XB) * Y])
            cells_2[z - 2] = delta[2 * Y : (2 + XB) * Y]
    for z in range(6):
        back = convolved(planes(delta_2, z), weights_t[1], False)
        pre = pre_own[z - 2] if z in (2, 3) else pre_1[z + 2]
        delta = (back * sigmoid(pre[2 * Y : (XW - 4) * Y])).astype(BF).astype(F32)
        store_taps(delta_1, z, delta)
        if 1 <= z < 5:
            cells_3[z - 1] = delta[Y : (1 + XB) * Y]
    for z in range(4):
        cells_1[z] = convolved(planes(delta_1, z), weights_t[0], False)

    count = ZB * XB * Y
    row = lax.broadcasted_iota(jnp.int32, (count, count // 2), 0)
    col = lax.broadcasted_iota(jnp.int32, (count, count // 2), 1)
    y = row % Y - half * (Y // 2)
    order = (y // 2) * 64 + (row // (XB * Y)) * 16 + (y % 2) * XB + (row // Y) % XB
    inside = (y >= 0) & (y < Y // 2)
    reorder = jnp.where(inside & (order == col), 1.0, 0.0).astype(BF)
    for at, cells in enumerate((cells_0, cells_1)):
        flat = jnp.transpose(cells[...].reshape(count, 128))[0:C, :].astype(BF)
        flat = jnp.dot(flat, reorder, preferred_element_type=F32).astype(BF)
        for to in range(SYH):
            first = QUARTER + at * 64
            out_ref[to, :, first : first + 64] = flat[:, to * 64 : to * 64 + 64]
    for base, cells, source, at in ((0, cells_3, field_rows, 3), (HALF, cells_2, act_rows, 2)):
        flat = jnp.transpose(cells[...].reshape(count, 128))[0:C, :].astype(BF)
        for b in range(3):
            for c in range(3):
                near = slice((at + c) * Y, (at + c + XB) * Y)
                near = jnp.concatenate([source(at + b + z, near) for z in range(ZB)], axis=0)
                sums = jnp.dot(flat, near, preferred_element_type=F32).astype(BF)
                for a in range(3):
                    first = base + tap_column(a, b, c)
                    to, first = first // QUARTER, first % QUARTER
                    out_ref[to, :, first : first + C] = sums[:, a * C : a * C + C]
        out_ref[(base + COLUMNS) // QUARTER, :, (base + COLUMNS) % QUARTER : QUARTER] = jnp.zeros(
            (C, HALF - COLUMNS), BF
        )


def split_kernel(in_ref, out_ref):
    for to in range(4):
        wide = min(PIECE, QUARTER - to * PIECE)
        lanes = slice(to * PIECE, to * PIECE + wide)
        total = in_ref[0, :, lanes].astype(F32)
        for k in range(1, BLOCKS):
            total = total + in_ref[k, :, lanes].astype(F32)
        out_ref[to, :, 0:wide] = total.astype(BF)
        if wide < PIECE:
            out_ref[to, :, wide:PIECE] = jnp.zeros((16, PIECE - wide), BF)


def sum_kernel(in_ref, out_ref):
    total = in_ref[0].astype(F32)
    for k in range(1, in_ref.shape[0]):
        total = total + in_ref[k].astype(F32)
    total = total.astype(BF)
    for k in range(out_ref.shape[0]):
        out_ref[k] = total


def finish_kernel(factor, in_ref, shares_ref, result_ref, grad_input_ref, first_ref, second_ref, held):
    for base, ref in ((0, first_ref), (8, second_ref)):
        for k in range(8):
            first = (k // 4) * QUARTER + (k % 4) * PIECE
            wide = min(PIECE, QUARTER - (k % 4) * PIECE, COLUMNS - first)
            ref[:, first : first + wide] = in_ref[base + k, :, 0:wide].astype(F32) * factor
    blocks = [shares_ref[k, :, QUARTER : QUARTER + 128].astype(F32) for k in range(BLOCKS)]
    slot = lanes_of((16, 128)) // XB
    for bit in (1, 2, 4, 8):
        clear = slot & bit == 0
        blocks = [
            jnp.where(clear, turned(blocks[k - bit], -bit * XB), blocks[k])
            if k & bit
            else jnp.where(clear, blocks[k], turned(blocks[k + bit], bit * XB))
            for k in range(BLOCKS)
        ]
    for at, ref in enumerate((result_ref, grad_input_ref)):
        for z in range(ZB):
            for yy in range(2):
                held[at, pl.ds(yy * ZB + z, 16, stride=8), :] = blocks[at * 8 + z * 2 + yy]
        ref[...] = held[at].astype(BF)


def body(volume, first_filters, second_filters, cotangent):
    shape = jax.ShapeDtypeStruct
    factor = float(SY * volume.shape[1] * SZ * volume.shape[2] * volume.shape[3]) ** -0.5
    with jax.named_scope("halves_exchange"):
        near = jnp.concatenate([volume.reshape(128, 128), cotangent.reshape(128, 128)], axis=0)
        far = lax.ppermute(near, "sy", [(i, (i + SYH) % SY) for i in range(SY)])
    with jax.named_scope("pack_windows"):
        packed = pl.pallas_call(
            pack_kernel,
            out_shape=shape((BLOCKS, 64, 128), BF),
            scratch_shapes=[pltpu.VMEM((512, 128), F32)],
            compiler_params=PARAMS,
            cost_estimate=pl.CostEstimate(flops=40_000_000_000, bytes_accessed=1_000_000, transcendentals=0),
        )(near, far)
    with jax.named_scope("filters_exchange"):
        filters = jnp.broadcast_to(jnp.stack([first_filters, second_filters]), (FILT, 2, 16, COLUMNS))
        filters = lax.all_to_all(filters, "filt", 0, 0, tiled=True)
        packed, filters = lax.optimization_barrier((packed, filters))
    with jax.named_scope("windows_exchange"):
        windows = lax.all_to_all(packed, ("sy", "filt"), 0, 0, tiled=True, axis_index_groups=SAME_HALF)
    with jax.named_scope("unpack_windows"):
        own = call(unpack_kernel, shape((ZB * PLANE, 128), BF), [pltpu.VMEM((ZB * PLANE, 128), F32)], windows)
    with jax.named_scope("z_rim_exchange"):
        below = lax.ppermute(own, PENCIL, along_z(1))
        above = lax.ppermute(own, PENCIL, along_z(-1))
    with jax.named_scope("prepare"):
        prepared = call(
            prepare_kernel,
            (
                shape((2, 256, 768), BF), shape((2, 768, 256), BF), shape((ZB, PLANE, 256), BF),
                shape((2, (XW - 2) * Y, 128), F32), shape((2, (XW - 2) * Y, 256), BF),
            ),
            [],
            own, filters,
        )
    with jax.named_scope("layers"):
        partial = call(
            main_kernel,
            shape((SYH, C, QUARTER + 128), BF),
            [
                pltpu.VMEM((8, XW * Y, 256), BF),
                pltpu.VMEM((10, (XW - 2) * Y, 256), BF),
                pltpu.VMEM((8, (XW - 4) * Y, 256), BF),
                pltpu.VMEM((6, (XW - 6) * Y, 256), BF),
                pltpu.VMEM((10, (XW - 2) * Y, 128), F32),
                pltpu.VMEM((ZB, XB * Y, 128), F32),
                pltpu.VMEM((ZB, XB * Y, 128), F32),
                pltpu.VMEM((ZB, XB * Y, 128), F32),
                pltpu.VMEM((ZB, XB * Y, 128), F32),
            ],
            below, own, above, *prepared,
        )
    with jax.named_scope("blocks_exchange"):
        shares = partial.reshape(BLOCKS, 16, QUARTER + 128)
        shares = lax.all_to_all(shares, ("sy", "filt"), 0, 0, tiled=True, axis_index_groups=SAME_HALF)
    with jax.named_scope("split_shares"):
        pieces = call(split_kernel, shape((4, 16, PIECE), BF), [], shares)
    with jax.named_scope("near_sum_exchange"):
        pieces = lax.all_to_all(pieces, PENCIL, 0, 0, tiled=True, axis_index_groups=FOURS)
        pieces = call(sum_kernel, shape((4, 16, PIECE), BF), [], pieces)
    with jax.named_scope("far_sum_exchange"):
        pieces = lax.all_to_all(pieces, PENCIL, 0, 0, tiled=True, axis_index_groups=FAR_FOURS)
        pieces = call(sum_kernel, shape((16, 16, PIECE), BF), [], pieces)
    with jax.named_scope("spread_exchange"):
        pieces = lax.all_to_all(pieces, PENCIL, 0, 0, tiled=True, axis_index_groups=SIXTEENS)
    with jax.named_scope("finish"):
        result, grad_input, first_grad, second_grad = call(
            lambda *refs: finish_kernel(factor, *refs),
            (
                shape((128, 128), BF), shape((128, 128), BF),
                shape((16, COLUMNS), F32), shape((16, COLUMNS), F32),
            ),
            [pltpu.VMEM((2, 128, 128), F32)],
            pieces, shares,
        )
    return (result.reshape(volume.shape), grad_input.reshape(volume.shape), first_grad, second_grad)


def solution(mesh):
    return jax.shard_map(
        body,
        mesh=mesh,
        in_specs=(
            P("filt", "sy", "sz", None),
            P("filt", None),
            P("filt", None),
            P("filt", "sy", "sz", None),
        ),
        out_specs=(
            P("filt", "sy", "sz", None),
            P("filt", "sy", "sz", None),
            P("filt", None),
            P("filt", None),
        ),
        check_vma=False,
    )
```

```python
import jax
import jax.numpy as jnp
from jax import lax
from jax.experimental import pallas as pl
from jax.experimental.pallas import tpu as pltpu
from jax.sharding import PartitionSpec as P

BF = jnp.bfloat16
F32 = jnp.float32
C = 64
Y = 16
SY = 8
SZ = 16
FILT = 4
SYH = SY // 2
ZB = 4
XB = 8
RIM = 4
XW = XB + 2 * RIM
PLANE = XW * Y
BLOCKS = SYH * FILT
HALF = 28 * C
GRADS = 2 * HALF
QUARTER = GRADS // SYH
PIECE = 256
COLUMNS = 27 * C
PARAMS = pltpu.CompilerParams(vmem_limit_bytes=48 * 1024 * 1024)


def at_device(half, y, z, core):
    return (half * SYH + y) * SZ + z * 2 + core


PENCIL = ("sy", "sz")
HALVES, PAIRS, CORES = range(2), range(SZ // 4), range(2)
SAME_HALF = [[half * BLOCKS + i for i in range(BLOCKS)] for half in HALVES]
FOURS = [
    [at_device(half, y, 2 * pair + odd, core) for odd in HALVES for core in CORES]
    for half in HALVES for y in range(SYH) for pair in PAIRS
]
FAR_FOURS = [
    [at_device(half, y, 2 * pair + odd, core) for pair in PAIRS]
    for half in HALVES for y in range(SYH) for odd in HALVES for core in CORES
]
SIXTEENS = [
    [at_device(half, y, 2 * pair + odd, core) for y in range(SYH) for odd in HALVES for core in CORES]
    for half in HALVES for pair in PAIRS
]


def along_z(step):
    pairs = []
    for half in HALVES:
        for y in range(SYH):
            for z in range(SZ):
                to = (half * SZ + z + step) % (2 * SZ)
                pairs.append((half * SYH * SZ + y * SZ + z, (to // SZ) * SYH * SZ + y * SZ + to % SZ))
    return pairs


def lanes_of(shape):
    return lax.broadcasted_iota(jnp.int32, shape, len(shape) - 1)


def turned(x, shift):
    return pltpu.roll(x, shift % x.shape[-1], x.ndim - 1)


def call(kernel, out_shape, scratch, *args):
    return pl.pallas_call(
        kernel, out_shape=out_shape, scratch_shapes=scratch, compiler_params=PARAMS
    )(*args)


def pack_kernel(near_ref, far_ref, out_ref, held):
    lower = lax.axis_index("sy") < SYH
    near, far = near_ref[...].astype(F32), far_ref[...].astype(F32)
    held[0:256, :] = jnp.where(lower, near, far)
    held[256:512, :] = jnp.where(lower, far, near)
    rows = [held[pl.ds(yz, 64, stride=8), :] for yz in range(8)]
    slot = lanes_of((64, 128)) // 16
    for k in range(BLOCKS):
        total = turned(rows[0], RIM - XB * k)
        for yz in range(1, 8):
            total = jnp.where(slot == yz, turned(rows[yz], 16 * yz + RIM - XB * k), total)
        out_ref[k] = total.astype(BF)


def unpack_kernel(in_ref, out_ref, held):
    for sy in range(SY):
        top = (sy // SYH) * 32
        block = jnp.concatenate(
            [
                in_ref[(sy % SYH) * FILT + f, top + 16 * vc : top + 16 * vc + 16, :]
                for vc in range(2) for f in range(FILT)
            ],
            axis=0,
        )
        flipped = jnp.transpose(block.astype(F32))
        for yy in range(2):
            for z in range(ZB):
                first = (yy * ZB + z) * XW
                held[pl.ds(z * PLANE + 2 * sy + yy, XW, stride=Y), :] = flipped[first : first + XW, :]
    out_ref[...] = held[...].astype(BF)


def y_taps(x):
    cells = x.shape[0] // Y
    split = x.reshape(cells, Y, 128)
    before = pltpu.roll(split, 1, 1).reshape(x.shape)
    after = pltpu.roll(split, Y - 1, 1).reshape(x.shape)
    return before, after


def store_taps(ref, z, x):
    before, after = y_taps(x)
    low = lanes_of(x.shape) < C
    ref[z, :, 0:128] = jnp.where(low, before, x).astype(BF)
    ref[z, :, 128:256] = after.astype(BF)


def store_field(ref, at, slab_ref, z):
    x = slab_ref[z * PLANE : (z + 1) * PLANE, :].astype(F32)
    before, after = y_taps(x)
    low = lanes_of(x.shape) < C
    ref[at, :, 0:128] = jnp.where(low, before, turned(x, C)).astype(BF)
    ref[at, :, 128:256] = after.astype(BF)


def softplus(x):
    return jnp.maximum(x, 0.0) + jnp.log1p(jnp.exp(-jnp.abs(x)))


def sigmoid(x):
    e = jnp.exp(-jnp.abs(x))
    return jnp.where(x >= 0, 1.0, e) / (1.0 + e)


def tap_column(a, b, c):
    return (9 * a + 3 * b + c) * C


def filter_block(filters_ref, layer, f, a, b, c):
    first = tap_column(a, b, c)
    return filters_ref[f, layer, :, first : first + C]


def fill_forward(ref, filters_ref, layer):
    ref[...] = jnp.zeros_like(ref)
    for b in range(3):
        for a in range(3):
            for at, c in ((0, 0), (1, 1), (2, 2), (3, 2)):
                for f in range(FILT):
                    row = at * C + f * 16
                    ref[row : row + 16, b * 256 + a * C : b * 256 + a * C + C] = filter_block(
                        filters_ref, layer, f, a, b, c
                    )


def fill_backward(ref, filters_ref, layer):
    ref[...] = jnp.zeros_like(ref)
    for b in range(3):
        for a in range(3):
            for at, c in ((0, 0), (1, 1), (2, 2), (3, 2)):
                for f in range(FILT):
                    row = b * 256 + a * C + f * 16
                    ref[row : row + 16, at * C : at * C + C] = filter_block(
                        filters_ref, layer, f, 2 - a, 2 - b, 2 - c
                    )


def convolved(planes, weights, transposed):
    rows = planes[0].shape[0]
    planes = jnp.concatenate(planes, axis=1)
    dims = (((1,), (1 if transposed else 0,)), ((), ()))
    sums = lax.dot_general(planes, weights, dims, preferred_element_type=F32)
    left, right = sums[:, 0:128], sums[:, 128:256]
    swapped = turned(left, C)
    kept = rows - 2 * Y
    low = lanes_of((kept, 128)) < C
    return (
        jnp.where(
            low,
            left[0:kept] + swapped[Y : Y + kept],
            left[Y : Y + kept] + swapped[0:kept],
        )
        + right[2 * Y : 2 * Y + kept]
    )


def prepare_kernel(own_ref, filters_ref, weights, weights_t, field, pre_own, act_own):
    for layer in range(2):
        fill_forward(weights.at[layer], filters_ref, layer)
        fill_backward(weights_t.at[layer], filters_ref, layer)
    for z in range(ZB):
        store_field(field, z, own_ref, z)
    for at in range(2):
        pre = convolved([field[at + b] for b in range(3)], weights[0], True)
        pre_own[at] = pre
        store_taps(act_own, at, softplus(pre).astype(BF).astype(F32))


def main_kernel(
    below_ref, own_ref, above_ref, weights, weights_t, field_own, pre_own, act_own, out_ref,
    field, act, delta_2, delta_1, pre_1, cells_0, cells_1, cells_2, cells_3,
):
    half = lax.axis_index("sy") // SYH
    slabs = (below_ref, own_ref, above_ref)

    def slab_rows(z, first, count):
        start = (z % ZB) * PLANE + first
        return slabs[z // ZB][start : start + count, :].astype(F32)

    def field_rows(z, rows):
        if ZB <= z < 2 * ZB:
            return field_own[z - ZB, rows, :]
        return field[z if z < ZB else z - ZB, rows, :]

    def planes(ref, z):
        return [ref[z + b] for b in range(3)]

    for z in range(ZB):
        store_field(field, z, below_ref, z)
        store_field(field, ZB + z, above_ref, z)
    def act_rows(z, rows):
        return act_own[z - 4, rows, :] if z in (4, 5) else act[z, rows, :]

    for z in (0, 1, 2, 3, 6, 7, 8, 9):
        pre = convolved([field_rows(z + b, slice(0, PLANE)) for b in range(3)], weights[0], True)
        if 2 <= z < 8:
            pre_1[z] = pre
        store_taps(act, z, softplus(pre).astype(BF).astype(F32))
    for z in range(8):
        pre = convolved([act_rows(z + b, slice(None)) for b in range(3)], weights[1], True)
        cotangent = slab_rows(z + 2, 2 * Y, (XW - 4) * Y)
        low = lanes_of(cotangent.shape) < C
        cotangent = jnp.where(low, turned(cotangent, C), cotangent)
        delta = (cotangent * sigmoid(pre)).astype(BF).astype(F32)
        store_taps(delta_2, z, delta)
        if 2 <= z < 6:
            cells_0[z - 2] = softplus(pre[2 * Y : (2 + XB) * Y])
            cells_2[z - 2] = delta[2 * Y : (2 + XB) * Y]
    for z in range(6):
        back = convolved(planes(delta_2, z), weights_t[1], False)
        pre = pre_own[z - 2] if z in (2, 3) else pre_1[z + 2]
        delta = (back * sigmoid(pre[2 * Y : (XW - 4) * Y])).astype(BF).astype(F32)
        store_taps(delta_1, z, delta)
        if 1 <= z < 5:
            cells_3[z - 1] = delta[Y : (1 + XB) * Y]
    for z in range(4):
        cells_1[z] = convolved(planes(delta_1, z), weights_t[0], False)

    count = ZB * XB * Y
    row = lax.broadcasted_iota(jnp.int32, (count, count // 2), 0)
    col = lax.broadcasted_iota(jnp.int32, (count, count // 2), 1)
    y = row % Y - half * (Y // 2)
    order = (y // 2) * 64 + (row // (XB * Y)) * 16 + (y % 2) * XB + (row // Y) % XB
    inside = (y >= 0) & (y < Y // 2)
    reorder = jnp.where(inside & (order == col), 1.0, 0.0).astype(BF)
    for at, cells in enumerate((cells_0, cells_1)):
        flat = jnp.transpose(cells[...].reshape(count, 128))[0:C, :].astype(BF)
        flat = jnp.dot(flat, reorder, preferred_element_type=F32).astype(BF)
        for to in range(SYH):
            first = QUARTER + at * 64
            out_ref[to, :, first : first + 64] = flat[:, to * 64 : to * 64 + 64]
    for base, cells, source, at in ((0, cells_3, field_rows, 3), (HALF, cells_2, act_rows, 2)):
        flat = jnp.transpose(cells[...].reshape(count, 128))[0:C, :].astype(BF)
        for b in range(3):
            for c in range(3):
                near = slice((at + c) * Y, (at + c + XB) * Y)
                near = jnp.concatenate([source(at + b + z, near) for z in range(ZB)], axis=0)
                sums = jnp.dot(flat, near, preferred_element_type=F32).astype(BF)
                for a in range(3):
                    first = base + tap_column(a, b, c)
                    to, first = first // QUARTER, first % QUARTER
                    out_ref[to, :, first : first + C] = sums[:, a * C : a * C + C]
        out_ref[(base + COLUMNS) // QUARTER, :, (base + COLUMNS) % QUARTER : QUARTER] = jnp.zeros(
            (C, HALF - COLUMNS), BF
        )


def split_kernel(in_ref, out_ref):
    for to in range(4):
        wide = min(PIECE, QUARTER - to * PIECE)
        lanes = slice(to * PIECE, to * PIECE + wide)
        total = in_ref[0, :, lanes].astype(F32)
        for k in range(1, BLOCKS):
            total = total + in_ref[k, :, lanes].astype(F32)
        out_ref[to, :, 0:wide] = total.astype(BF)
        if wide < PIECE:
            out_ref[to, :, wide:PIECE] = jnp.zeros((16, PIECE - wide), BF)


def sum_kernel(in_ref, out_ref):
    total = in_ref[0].astype(F32)
    for k in range(1, in_ref.shape[0]):
        total = total + in_ref[k].astype(F32)
    total = total.astype(BF)
    for k in range(out_ref.shape[0]):
        out_ref[k] = total


def finish_kernel(factor, in_ref, shares_ref, result_ref, grad_input_ref, first_ref, second_ref, held):
    for base, ref in ((0, first_ref), (8, second_ref)):
        for k in range(8):
            first = (k // 4) * QUARTER + (k % 4) * PIECE
            wide = min(PIECE, QUARTER - (k % 4) * PIECE, COLUMNS - first)
            ref[:, first : first + wide] = in_ref[base + k, :, 0:wide].astype(F32) * factor
    blocks = [shares_ref[k, :, QUARTER : QUARTER + 128].astype(F32) for k in range(BLOCKS)]
    slot = lanes_of((16, 128)) // XB
    for bit in (1, 2, 4, 8):
        clear = slot & bit == 0
        blocks = [
            jnp.where(clear, turned(blocks[k - bit], -bit * XB), blocks[k])
            if k & bit
            else jnp.where(clear, blocks[k], turned(blocks[k + bit], bit * XB))
            for k in range(BLOCKS)
        ]
    for at, ref in enumerate((result_ref, grad_input_ref)):
        for z in range(ZB):
            for yy in range(2):
                held[at, pl.ds(yy * ZB + z, 16, stride=8), :] = blocks[at * 8 + z * 2 + yy]
        ref[...] = held[at].astype(BF)


def body(volume, first_filters, second_filters, cotangent):
    shape = jax.ShapeDtypeStruct
    factor = float(SY * volume.shape[1] * SZ * volume.shape[2] * volume.shape[3]) ** -0.5
    with jax.named_scope("halves_exchange"):
        near = jnp.concatenate([volume.reshape(128, 128), cotangent.reshape(128, 128)], axis=0)
        far = lax.ppermute(near, "sy", [(i, (i + SYH) % SY) for i in range(SY)])
    with jax.named_scope("pack_windows"):
        packed = pl.pallas_call(
            pack_kernel,
            out_shape=shape((BLOCKS, 64, 128), BF),
            scratch_shapes=[pltpu.VMEM((512, 128), F32)],
            compiler_params=PARAMS,
            cost_estimate=pl.CostEstimate(flops=40_000_000_000, bytes_accessed=1_000_000, transcendentals=0),
        )(near, far)
    with jax.named_scope("filters_exchange"):
        filters = jnp.broadcast_to(jnp.stack([first_filters, second_filters]), (FILT, 2, 16, COLUMNS))
        filters = lax.all_to_all(filters, "filt", 0, 0, tiled=True)
        packed, filters = lax.optimization_barrier((packed, filters))
    with jax.named_scope("windows_exchange"):
        windows = lax.all_to_all(packed, ("sy", "filt"), 0, 0, tiled=True, axis_index_groups=SAME_HALF)
    with jax.named_scope("unpack_windows"):
        own = call(unpack_kernel, shape((ZB * PLANE, 128), BF), [pltpu.VMEM((ZB * PLANE, 128), F32)], windows)
    with jax.named_scope("z_rim_exchange"):
        below = lax.ppermute(own, PENCIL, along_z(1))
        above = lax.ppermute(own, PENCIL, along_z(-1))
    with jax.named_scope("prepare"):
        prepared = call(
            prepare_kernel,
            (
                shape((2, 256, 768), BF), shape((2, 768, 256), BF), shape((ZB, PLANE, 256), BF),
                shape((2, (XW - 2) * Y, 128), F32), shape((2, (XW - 2) * Y, 256), BF),
            ),
            [],
            own, filters,
        )
    with jax.named_scope("layers"):
        partial = call(
            main_kernel,
            shape((SYH, C, QUARTER + 128), BF),
            [
                pltpu.VMEM((8, XW * Y, 256), BF),
                pltpu.VMEM((10, (XW - 2) * Y, 256), BF),
                pltpu.VMEM((8, (XW - 4) * Y, 256), BF),
                pltpu.VMEM((6, (XW - 6) * Y, 256), BF),
                pltpu.VMEM((10, (XW - 2) * Y, 128), F32),
                pltpu.VMEM((ZB, XB * Y, 128), F32),
                pltpu.VMEM((ZB, XB * Y, 128), F32),
                pltpu.VMEM((ZB, XB * Y, 128), F32),
                pltpu.VMEM((ZB, XB * Y, 128), F32),
            ],
            below, own, above, *prepared,
        )
    with jax.named_scope("blocks_exchange"):
        shares = partial.reshape(BLOCKS, 16, QUARTER + 128)
        shares = lax.all_to_all(shares, ("sy", "filt"), 0, 0, tiled=True, axis_index_groups=SAME_HALF)
    with jax.named_scope("split_shares"):
        pieces = call(split_kernel, shape((4, 16, PIECE), BF), [], shares)
    with jax.named_scope("near_sum_exchange"):
        pieces = lax.all_to_all(pieces, PENCIL, 0, 0, tiled=True, axis_index_groups=FOURS)
        pieces = call(sum_kernel, shape((4, 16, PIECE), BF), [], pieces)
    with jax.named_scope("far_sum_exchange"):
        pieces = lax.all_to_all(pieces, PENCIL, 0, 0, tiled=True, axis_index_groups=FAR_FOURS)
        pieces = call(sum_kernel, shape((16, 16, PIECE), BF), [], pieces)
    with jax.named_scope("spread_exchange"):
        pieces = lax.all_to_all(pieces, PENCIL, 0, 0, tiled=True, axis_index_groups=SIXTEENS)
    with jax.named_scope("finish"):
        result, grad_input, first_grad, second_grad = call(
            lambda *refs: finish_kernel(factor, *refs),
            (
                shape((128, 128), BF), shape((128, 128), BF),
                shape((16, COLUMNS), F32), shape((16, COLUMNS), F32),
            ),
            [pltpu.VMEM((2, 128, 128), F32)],
            pieces, shares,
        )
    return (result.reshape(volume.shape), grad_input.reshape(volume.shape), first_grad, second_grad)


def solution(mesh):
    return jax.shard_map(
        body,
        mesh=mesh,
        in_specs=(
            P("filt", "sy", "sz", None),
            P("filt", None),
            P("filt", None),
            P("filt", "sy", "sz", None),
        ),
        out_specs=(
            P("filt", "sy", "sz", None),
            P("filt", "sy", "sz", None),
            P("filt", None),
            P("filt", None),
        ),
        check_vma=False,
    )
```
